128 devices in a mesh: group: 4 (over z), dev: 32 (over x, y, core).
Axes of the slice: x: 4, y: 4, z: 4, core: 2. Of those that a mesh axis runs over, the one named last changes fastest.
Arguments:
- geometry: float32 [8192, 4, 256], P(('group', 'dev'))
- charges: float32 [8192, 16, 256], P(('group', 'dev')), may hold values from -6 to 6
- leaf_cluster_basis: float32 [8192, 32, 256], P(('group', 'dev')), may hold values from -1 to 1
- near_list: int32 [8192, 12], P(('group', 'dev')), may hold values from 0 to 8191, as said below
- near_count: int32 [8192], P(('group', 'dev')), may hold values from 1 to 12, as said below
- leaf_transfer: float32 [1024, 8, 32, 32], P(('group', 'dev')), may hold values from -0.375 to 0.375
- box_transfer: float32 [128, 8, 32, 32], P(('group', 'dev')), may hold values from -0.375 to 0.375
- box_far_list: int32 [1024, 16], P(('group', 'dev')), may hold values from 0 to 1023, as said below
- box_coupling: float32 [1024, 16, 32, 32], P(('group', 'dev')), may hold values from -0.25 to 0.25
- top_far_list: int32 [128, 16], P(('group', 'dev')), may hold values from 0 to 127, as said below
- top_coupling: float32 [128, 16, 32, 32], P(('group', 'dev')), may hold values from -0.25 to 0.25
Outputs:
- potential: float32 [8192, 16, 256], P(('group', 'dev'))
The draws below stay inside these ranges and needn't reach their ends.
Inputs may be any that keep to these rules, and one draw needn't show every extreme that they name: `near_list`: row i holds distinct leaves whose index differs from i by at most 32; its first entry is i itself. `near_count`: leaf 0 uses all 12 slots. `box_far_list`: row b holds 16 distinct boxes other than b. `top_far_list`: row a holds 16 distinct upper boxes other than a.
All inputs are finite; a program needn't handle non-finite values.
Results may differ from the reference program's by a relative error of at most 0.0003.
Values sent between devices are 32-bit elements; how exact they have to be, the bound alone decides.
A program may use at most 64 MiB of HBM per device.

```python
import math
import jax
import jax.numpy as jnp
from jax import lax

LEAF = 256
RANK = 32
RHS = 16
NEAR = 12
FAR = 16
LEAF_DEV = 64
NEAR_REACH = 32
LEAVES = 8192
BOX1 = 1024
BOX2 = 128


def draw_geometry(key, part):
    key = jax.random.fold_in(key, 11)
    key_panels = jax.random.fold_in(key, 1)
    key_areas = jax.random.fold_in(key, 2)
    position = jnp.arange(LEAVES).astype(jnp.float32)
    centers = jnp.stack([0.025 * position, 0.1 * jnp.sin(0.05 * position), 0.1 * jnp.cos(0.05 * position)], axis=1)
    spread = 0.25
    areas = jnp.exp(jax.random.uniform(key_areas, (LEAVES, 1, LEAF), jnp.float32, jnp.log(0.02), jnp.log(0.2)))
    spots = centers[:, :, None] + jax.random.uniform(key_panels, (LEAVES, 3, LEAF), jnp.float32, -spread, spread)
    return jnp.concatenate([spots, areas], axis=1).astype(jnp.float32)


def draw_near_list(key, part):
    key = jax.random.fold_in(key, 12)
    key_order = jax.random.fold_in(key, 1)
    key_signs = jax.random.fold_in(key, 2)
    table = jnp.broadcast_to(jnp.arange(1, NEAR_REACH + 1, dtype=jnp.int32), (LEAVES, NEAR_REACH))
    offsets = jax.random.permutation(key_order, table, axis=1, independent=True)[:, :NEAR - 1]
    signs = jax.random.randint(key_signs, (LEAVES, NEAR - 1), 0, 2).astype(jnp.int32) * 2 - 1
    rows = jnp.arange(LEAVES, dtype=jnp.int32)[:, None]
    forward = rows + signs * offsets
    chosen = jnp.where((forward < 0) | (forward >= LEAVES), rows - signs * offsets, forward)
    return jnp.concatenate([rows, chosen], axis=1).astype(jnp.int32)


def draw_near_count(key, part):
    key = jax.random.fold_in(key, 13)
    key_caps = jax.random.fold_in(key, 1)
    key_counts = jax.random.fold_in(key, 2)
    caps = jax.random.randint(key_caps, (LEAVES // LEAF_DEV,), 3, NEAR + 1).astype(jnp.int32)
    spread_caps = jnp.repeat(caps, LEAF_DEV)
    counts = jax.random.randint(key_counts, (LEAVES,), 1, spread_caps + 1).astype(jnp.int32)
    counts = counts.at[0].set(NEAR)
    counts = counts.at[1].set(1)
    return counts.astype(jnp.int32)


def far_table(key, boxes):
    table = jnp.broadcast_to(jnp.arange(1, boxes, dtype=jnp.int32), (boxes, boxes - 1))
    offsets = jax.random.permutation(key, table, axis=1, independent=True)[:, :FAR]
    rows = jnp.arange(boxes, dtype=jnp.int32)[:, None]
    return ((rows + offsets) % boxes).astype(jnp.int32)


def draw_box_far_list(key, part):
    key = jax.random.fold_in(key, 14)
    return far_table(key, BOX1)


def draw_top_far_list(key, part):
    key = jax.random.fold_in(key, 15)
    return far_table(key, BOX2)


def shard_levels(rng, extent, shards, smallest, largest):
    gain = 1.0
    for dim, parts in shards:
        heights = jax.random.uniform(jax.random.fold_in(jax.random.fold_in(rng, 6), dim), (parts,), jnp.float32, smallest / len(shards), largest / len(shards))
        gain = gain * jnp.repeat(jnp.exp(heights), extent[dim] // parts).reshape((-1,) + (1,) * (len(extent) - 1 - dim))
    return gain


def bell_draw(stream_key, extent, width, most, cuts=(), kind=jnp.bfloat16):
    entries = jax.random.normal(stream_key, extent, jnp.float32) * width
    if len(cuts) > 0:
        entries = shard_levels(stream_key, extent, cuts, -0.22, 0.18) * entries
    return jnp.clip(entries, min=-most, max=most).astype(kind)


def setup_inputs(seed: int = 0) -> dict:
    key_of = jax.random.split(jax.random.key(seed), 12)
    return {
        "geometry": draw_geometry(jax.random.fold_in(key_of[11], 71), 0),
        "charges": bell_draw(key_of[1], (LEAVES, RHS, LEAF), 1.0, 6.0, ((0, 128),), jnp.float32),
        "leaf_cluster_basis": bell_draw(key_of[2], (LEAVES, RANK, LEAF), RANK ** -0.5, 1.0, ((0, 128),), jnp.float32),
        "near_list": draw_near_list(jax.random.fold_in(key_of[11], 71), 0),
        "near_count": draw_near_count(jax.random.fold_in(key_of[11], 71), 0),
        "leaf_transfer": bell_draw(key_of[5], (BOX1, 8, RANK, RANK), (8 * RANK) ** -0.5, 0.375, ((0, 128),), jnp.float32),
        "box_transfer": bell_draw(key_of[6], (BOX2, 8, RANK, RANK), (8 * RANK) ** -0.5, 0.375, ((0, 128),), jnp.float32),
        "box_far_list": draw_box_far_list(jax.random.fold_in(key_of[11], 71), 0),
        "box_coupling": bell_draw(key_of[8], (BOX1, FAR, RANK, RANK), (FAR * RANK) ** -0.5, 0.25, ((0, 128),), jnp.float32),
        "top_far_list": draw_top_far_list(jax.random.fold_in(key_of[11], 71), 0),
        "top_coupling": bell_draw(key_of[10], (BOX2, FAR, RANK, RANK), (FAR * RANK) ** -0.5, 0.25, ((0, 128),), jnp.float32),
    }


SOFTENING = 0.0025
FOUR_PI = 4.0 * math.pi

def near_blocks(target, source):
    squared = jnp.zeros((target.shape[0], target.shape[2], source.shape[2]), jnp.float32)
    for comp in range(3):
        apart = target[:, comp, :, None] - source[:, comp, None, :]
        squared = squared + apart * apart
    kernel = source[:, 3, None, :] / (FOUR_PI * jnp.sqrt(squared + SOFTENING))
    return jnp.einsum('npq,nsq->nsp', kernel, source[:, 4:, :], precision=lax.Precision.HIGHEST)

def reference(geometry, charges, leaf_cluster_basis, near_list, near_count, leaf_transfer, box_transfer, box_far_list, box_coupling, top_far_list, top_coupling):
    leaves = geometry.shape[0]
    panels = geometry.shape[2]
    stacked = jnp.concatenate([geometry, charges], axis=1)
    blocks_count = leaves // 8

    def one_block(operands):
        target, slot_lists, counts = operands
        running = jnp.zeros((8, RHS, panels), jnp.float32)
        for index_of_slot in range(NEAR):
            source = jnp.take(stacked, slot_lists[:, index_of_slot], axis=0)
            term = near_blocks(target, source)
            running = running + jnp.where((index_of_slot < counts)[:, None, None], term, 0.0)
        return running
    nearby_panels = lax.map(one_block, (geometry.reshape(blocks_count, 8, 4, panels), near_list.reshape(blocks_count, 8, NEAR), near_count.reshape(blocks_count, 8)))
    nearby_panels = nearby_panels.reshape(leaves, RHS, panels)
    finest_level = lax.Precision.HIGHEST
    leaf_moment_values = jnp.einsum('gvx,gfx->gfv', leaf_cluster_basis, charges, precision=finest_level)
    box_moments = jnp.einsum('bcsr,bcrt->bst', leaf_moment_values.reshape(BOX1, 8, RHS, RANK), leaf_transfer, precision=finest_level)
    top_moments = jnp.einsum('acsr,acrt->ast', box_moments.reshape(BOX2, 8, RHS, RANK), box_transfer, precision=finest_level)
    top_local = jnp.einsum('afsr,afrt->ast', jnp.take(top_moments, top_far_list, axis=0), top_coupling, precision=finest_level)
    box_far = jnp.einsum('bfsu,bfur->bsr', jnp.take(box_moments, box_far_list, axis=0), box_coupling, precision=finest_level)
    box_down = jnp.einsum('ast,acrt->acsr', top_local, box_transfer, precision=finest_level).reshape(BOX1, RHS, RANK)
    box_local = box_far + box_down
    leaf_local_expansion = jnp.einsum('bst,bcrt->bcsr', box_local, leaf_transfer, precision=finest_level).reshape(leaves, RHS, RANK)
    return nearby_panels + jnp.einsum('hmw,hwq->hmq', leaf_local_expansion, leaf_cluster_basis, precision=finest_level)
```

```python
import functools
import math

import jax
import jax.numpy as jnp
from jax import lax
from jax.experimental import pallas as pl
from jax.experimental.pallas import tpu as pltpu
from jax.sharding import PartitionSpec as P

SOFTENING = 0.0025
FOUR_PI = 4.0 * math.pi
AXES = ("group", "dev")

LEAF = 256
RANK = 32
RHS = 16
NEAR = 12
FAR = 16
REACH = 32
OWN = 64
WIDE = OWN + 2 * REACH
UNROLL = 12
FEATURES = 48
EXTENT = 8.0

f32 = jnp.float32
bf16 = jnp.bfloat16
NN = (((1,), (0,)), ((), ()))
NT = (((1,), (1,)), ((), ()))


def dot(a, b, dims):
    return lax.dot_general(a, b, dims, preferred_element_type=f32)


def halves(v):
    hi = v.astype(bf16)
    return hi, (v - hi.astype(f32)).astype(bf16)


def thirds(v):
    a = v.astype(bf16).astype(f32)
    b = (v - a).astype(bf16).astype(f32)
    return a, b, v - a - b


def dot3(a, b, dims):
    ah, al = halves(a)
    bh, bl = halves(b)
    rows = a.shape[0]
    both = dot(jnp.concatenate([ah, al], axis=0), bh, dims)
    return both[:rows] + both[rows:] + dot(ah, bl, dims)


def upward_kernel(charges, basis, leaf_transfer, box_transfer, out, moments):
    box = pl.program_id(0)
    parts = [dot3(charges[c], basis[c], NT) for c in range(8)]
    leaf_moments = jnp.concatenate(parts, axis=1)
    moments[box] = dot3(leaf_moments, leaf_transfer[...].reshape(8 * RANK, RANK), NN)

    @pl.when(box == 7)
    def _():
        boxes = jnp.concatenate([moments[b] for b in range(8)], axis=1)
        top = dot3(boxes, box_transfer[...].reshape(8 * RANK, RANK), NN)
        out[0, :, : 8 * RANK] = boxes
        out[0, :, 8 * RANK :] = jnp.concatenate([top, jnp.zeros((RHS, 128 - RANK), f32)], axis=1)


def upward(charges, basis, leaf_transfer, box_transfer):
    return pl.pallas_call(
        upward_kernel,
        grid=(8,),
        out_shape=jax.ShapeDtypeStruct((1, RHS, 8 * RANK + 128), f32),
        in_specs=[
            pl.BlockSpec((8, RHS, LEAF), lambda b: (b, 0, 0)),
            pl.BlockSpec((8, RANK, LEAF), lambda b: (b, 0, 0)),
            pl.BlockSpec((1, 8, RANK, RANK), lambda b: (b, 0, 0, 0)),
            pl.BlockSpec((1, 8, RANK, RANK), lambda b: (0, 0, 0, 0)),
        ],
        out_specs=pl.BlockSpec((1, RHS, 8 * RANK + 128), lambda b: (0, 0, 0)),
        scratch_shapes=[pltpu.VMEM((8, RHS, RANK), f32)],
        compiler_params=pltpu.CompilerParams(vmem_limit_bytes=16 * 2**20),
        cost_estimate=pl.CostEstimate(flops=10**8, bytes_accessed=5 * 10**6, transcendentals=0),
        name="upward",
    )(charges, basis, leaf_transfer, box_transfer)


def near_kernel(
    place, near_list, near_count, geometry, geo_before, geo_after, charges, ch_before, ch_after,
    out, geo, source, source_rows, target_rows, block_hi, block_lo, total, extent,
):
    me = place[0]
    offset = me * OWN - REACH
    geo[0:REACH] = geo_before[...]
    geo[REACH : REACH + OWN] = geometry[...]
    geo[REACH + OWN :] = geo_after[...]
    centre = jnp.broadcast_to(jnp.mean(geometry[OWN // 2], axis=1, keepdims=True), (4, LEAF))
    one = jnp.ones((1, LEAF), f32)
    rest = jnp.zeros((3, LEAF), f32)

    def squared_norm(v):
        return v[0:1] * v[0:1] + v[1:2] * v[1:2] + v[2:3] * v[2:3]

    def weigh(part, start):
        def leaf(n, carry):
            area = geo[start + n][3:4] * (1.0 / FOUR_PI)
            hi, lo = halves(part[n] * area)
            source[start + n] = jnp.concatenate([hi, lo], axis=0)
            return carry

        lax.fori_loop(0, part.shape[0], leaf, 0, unroll=8)

    weigh(ch_before, 0)
    weigh(charges, REACH)
    weigh(ch_after, REACH + OWN)

    def target(n, largest):
        v = geo[n + REACH] - centre
        norm = squared_norm(v)
        a, b, c = thirds(jnp.concatenate([v[0:3], one, norm + SOFTENING, rest], axis=0))
        target_rows[n] = jnp.concatenate([a, a, b, b, a, c], axis=0).astype(bf16)
        total[n] = jnp.zeros((RHS, LEAF), f32)
        return jnp.maximum(largest, norm)

    def neighbour(n, largest):
        v = geo[n] - centre
        norm = squared_norm(v)
        a, b, c = thirds(jnp.concatenate([-2.0 * v[0:3], norm, one, rest], axis=0))
        source_rows[n, :, :FEATURES] = jnp.concatenate([a, b, a, b, c, a], axis=0).astype(bf16).T
        leaf = offset + n
        held = (leaf >= 0) & (leaf < place[1])
        return jnp.maximum(largest, jnp.where(held, norm, 0.0))

    nothing = jnp.zeros((1, LEAF), f32)
    targets = lax.fori_loop(0, OWN, target, nothing, unroll=8)
    sources = lax.fori_loop(0, WIDE, neighbour, nothing, unroll=8)
    total[OWN] = jnp.zeros((RHS, LEAF), f32)
    extent[0] = jnp.max(targets) + jnp.max(sources)
    compact = extent[0] <= EXTENT

    @pl.when(compact)
    def _():
        pairs = lax.fori_loop(0, OWN, lambda n, s: s + near_count[n], 0)

        def after(leaf, slot):
            row = jnp.minimum(leaf, OWN - 1)
            more = slot + 1 < near_count[row]
            return jnp.where(more, leaf, jnp.minimum(leaf + 1, OWN)), jnp.where(more, slot + 1, 0)

        def fill(u, leaf, slot):
            row = jnp.minimum(leaf, OWN - 1)
            j = near_list[row, slot] - offset
            for q in range(0, LEAF, 128):
                entries = lax.rsqrt(dot(source_rows[j, q : q + 128, :FEATURES], target_rows[row], NN))
                hi, lo = halves(entries)
                block_hi[u, q : q + 128] = hi
                block_lo[u, q : q + 128] = lo
            return j

        def use(u, leaf, j):
            both = source[j]
            r = dot(both, block_hi[u], NN)
            total[leaf] = total[leaf] + (r[:RHS] + r[RHS:] + dot(both[:RHS], block_lo[u], NN))

        def round_of(state, use_old):
            leaf, slot = state[0], state[1]
            new = []
            for u in range(UNROLL):
                if use_old:
                    use(u, state[2 + 2 * u], state[3 + 2 * u])
                new += [leaf, fill(u, leaf, slot)]
                leaf, slot = after(leaf, slot)
            return (leaf, slot, *new)

        start = round_of((jnp.int32(0), jnp.int32(0)), False)
        lax.fori_loop(0, (pairs + UNROLL - 1) // UNROLL, lambda t, s: round_of(s, True), start)

    @pl.when(jnp.logical_not(compact))
    def _():
        def leaf_sum(n, carry):
            columns = geo[n + REACH].T

            def slot_sum(k, running):
                j = near_list[n, k] - offset
                v = geo[j]
                both = source[j]
                parts = []
                for p in range(0, LEAF, 128):
                    squared = jnp.full((128, LEAF), SOFTENING, f32)
                    for comp in range(3):
                        apart = columns[p : p + 128, comp : comp + 1] - v[comp : comp + 1]
                        squared = squared + apart * apart
                    hi, lo = halves(lax.rsqrt(squared))
                    r = dot(both, hi, NT)
                    parts.append(r[:RHS] + r[RHS:] + dot(both[:RHS], lo, NT))
                return running + jnp.concatenate(parts, axis=1)

            total[n] = lax.fori_loop(0, near_count[n], slot_sum, jnp.zeros((RHS, LEAF), f32))
            return carry

        lax.fori_loop(0, OWN, leaf_sum, 0)

    out[...] = total[0:OWN]


def near_field(place, near_list, near_count, *arrays):
    smem = pl.BlockSpec(memory_space=pltpu.SMEM)
    vmem = pl.BlockSpec(memory_space=pltpu.VMEM)
    return pl.pallas_call(
        near_kernel,
        out_shape=jax.ShapeDtypeStruct((OWN, RHS, LEAF), f32),
        in_specs=[smem] * 3 + [vmem] * 6,
        out_specs=vmem,
        scratch_shapes=[
            pltpu.VMEM((WIDE, 4, LEAF), f32),
            pltpu.VMEM((WIDE, 2 * RHS, LEAF), bf16),
            pltpu.VMEM((WIDE, LEAF, 128), bf16),
            pltpu.VMEM((OWN, FEATURES, LEAF), bf16),
            pltpu.VMEM((UNROLL, LEAF, LEAF), bf16),
            pltpu.VMEM((UNROLL, LEAF, LEAF), bf16),
            pltpu.VMEM((OWN + 1, RHS, LEAF), f32),
            pltpu.SMEM((1,), f32),
        ],
        compiler_params=pltpu.CompilerParams(vmem_limit_bytes=40 * 2**20),
        cost_estimate=pl.CostEstimate(flops=2 * 10**10, bytes_accessed=4 * 10**6, transcendentals=5 * 10**7),
        name="near_field",
    )(place, near_list, near_count, *arrays)


def downward_kernel(
    box_far_list, top_far_list, gathered, top_coupling, box_transfer, box_coupling, leaf_transfer, basis, near,
    out, box_down,
):
    box = pl.program_id(0)

    @pl.when(box == 0)
    def _():
        top_local = jnp.zeros((RHS, RANK), f32)
        for f in range(FAR):
            top = gathered[top_far_list[0, f], :, 8 * RANK : 8 * RANK + RANK]
            top_local = top_local + dot3(top, top_coupling[0, f], NN)
        down = dot3(top_local, box_transfer[...].reshape(8 * RANK, RANK), NT)
        for b in range(8):
            box_down[b] = down[:, b * RANK : (b + 1) * RANK]

    local = box_down[box]
    for f in range(FAR):
        far = box_far_list[box, f]
        lane = (far % 8) * RANK
        base = pl.multiple_of((lane // 128) * 128, 128)
        tile = gathered[far // 8, :, pl.ds(base, 128)]
        tile = pltpu.roll(tile, (128 - lane % 128) % 128, 1)
        local = local + dot3(tile[:, :RANK], box_coupling[0, f], NN)
    leaves = dot3(local, leaf_transfer[...].reshape(8 * RANK, RANK), NT)
    for c in range(8):
        out[c] = near[c] + dot3(leaves[:, c * RANK : (c + 1) * RANK], basis[c], NN)


def downward(box_far_list, top_far_list, gathered, top_coupling, box_transfer, box_coupling, leaf_transfer, basis, near):
    smem = pl.BlockSpec(memory_space=pltpu.SMEM)
    vmem = pl.BlockSpec(memory_space=pltpu.VMEM)
    return pl.pallas_call(
        downward_kernel,
        grid=(8,),
        out_shape=jax.ShapeDtypeStruct((OWN, RHS, LEAF), f32),
        in_specs=[
            smem,
            smem,
            vmem,
            vmem,
            vmem,
            pl.BlockSpec((1, FAR, RANK, RANK), lambda b: (b, 0, 0, 0)),
            pl.BlockSpec((1, 8, RANK, RANK), lambda b: (b, 0, 0, 0)),
            pl.BlockSpec((8, RANK, LEAF), lambda b: (b, 0, 0)),
            pl.BlockSpec((8, RHS, LEAF), lambda b: (b, 0, 0)),
        ],
        out_specs=pl.BlockSpec((8, RHS, LEAF), lambda b: (b, 0, 0)),
        scratch_shapes=[pltpu.VMEM((8, RHS, RANK), f32)],
        compiler_params=pltpu.CompilerParams(vmem_limit_bytes=24 * 2**20),
        name="downward",
    )(box_far_list, top_far_list, gathered, top_coupling, box_transfer, box_coupling, leaf_transfer, basis, near)


def on_device(
    geometry,
    charges,
    leaf_cluster_basis,
    near_list,
    near_count,
    leaf_transfer,
    box_transfer,
    box_far_list,
    box_coupling,
    top_far_list,
    top_coupling,
):
    size = lax.axis_size(AXES)
    up = [(i, i + 1) for i in range(size - 1)]
    down = [(i + 1, i) for i in range(size - 1)]
    geo_before = lax.ppermute(geometry[OWN - REACH :], AXES, up)
    geo_after = lax.ppermute(geometry[:REACH], AXES, down)
    ch_before = lax.ppermute(charges[OWN - REACH :], AXES, up)
    ch_after = lax.ppermute(charges[:REACH], AXES, down)
    moments = upward(charges, leaf_cluster_basis, leaf_transfer, box_transfer)
    gathered = lax.all_gather(moments, AXES, axis=0, tiled=True)
    place = jnp.stack([lax.axis_index(AXES), jnp.int32(size * OWN)]).astype(jnp.int32)
    near = near_field(
        place, near_list, near_count, geometry, geo_before, geo_after, charges, ch_before, ch_after
    )
    return downward(
        box_far_list, top_far_list, gathered, top_coupling, box_transfer, box_coupling, leaf_transfer,
        leaf_cluster_basis, near,
    )


def solution(mesh):
    wide = P(AXES)
    return jax.shard_map(on_device, mesh=mesh, in_specs=(wide,) * 11, out_specs=wide, check_vma=False)
```

```python
import functools
import math

import jax
import jax.numpy as jnp
from jax import lax
from jax.experimental import pallas as pl
from jax.experimental.pallas import tpu as pltpu
from jax.sharding import PartitionSpec as P

SOFTENING = 0.0025
FOUR_PI = 4.0 * math.pi
AXES = ("group", "dev")

LEAF = 256
RANK = 32
RHS = 16
NEAR = 12
FAR = 16
REACH = 32
OWN = 64
WIDE = OWN + 2 * REACH
UNROLL = 12
VMEM = 60 * 2**20
FEATURES = 48
EXTENT = 8.0

f32 = jnp.float32
bf16 = jnp.bfloat16
NN = (((1,), (0,)), ((), ()))
NT = (((1,), (1,)), ((), ()))


def dot(a, b, dims):
    return lax.dot_general(a, b, dims, preferred_element_type=f32)


def halves(v):
    hi = v.astype(bf16)
    return hi, (v - hi.astype(f32)).astype(bf16)


def thirds(v):
    a = v.astype(bf16).astype(f32)
    b = (v - a).astype(bf16).astype(f32)
    return a, b, v - a - b


def dot3(a, b, dims):
    ah, al = halves(a)
    bh, bl = halves(b)
    rows = a.shape[0]
    both = dot(jnp.concatenate([ah, al], axis=0), bh, dims)
    return both[:rows] + both[rows:] + dot(ah, bl, dims)


ORDERS = ((0, 1, 2), (1, 2, 0), (2, 0, 1))


def coordinates(device):
    return (device // 32, (device // 2) % 4, (device // 8) % 4), device % 2


def row_in(part, chip, core):
    first, second, third = (chip[axis] for axis in ORDERS[part])
    return ((core * 4 + third) * 4 + second) * 4 + first


def exchange_kernel(
    geometry, charges_far, charges, basis, leaf_transfer, box_transfer,
    gathered, geo_halo, ch_halo, moments, send, receive, halo_send, halo_receive,
):
    me = lax.axis_index("group") * 32 + lax.axis_index("dev")
    chip, core = coordinates(me)

    def device(chip, core):
        return (chip[0], (chip[2] * 4 + chip[1]) * 2 + core)

    def peer(axis, step):
        moved = list(chip)
        moved[axis] = (chip[axis] + step) % 4
        return device(moved, core)

    sibling = device(chip, 1 - core)
    above = (me + 1) % 128
    below = (me + 127) % 128
    above = (above // 32, above % 32)
    below = (below // 32, below % 32)

    barrier = pltpu.get_barrier_semaphore()
    partners = [peer(axis, step) for axis in range(3) for step in (1, 2, 3)] + [sibling, above, below]
    for partner in partners:
        pl.semaphore_signal(barrier, inc=1, device_id=partner, device_id_type=pl.DeviceIdType.MESH)

    def remote(source, target, sent, received, partner):
        return pltpu.make_async_remote_copy(
            src_ref=source, dst_ref=target, send_sem=sent, recv_sem=received,
            device_id=partner, device_id_type=pl.DeviceIdType.MESH,
        )

    def box_moments(box, carry):
        parts = [dot3(charges[box * 8 + c], basis[box * 8 + c], NT) for c in range(8)]
        transfer = leaf_transfer[box].reshape(8 * RANK, RANK)
        moments[box] = dot3(jnp.concatenate(parts, axis=1), transfer, NN)
        return carry

    box_moments(0, 0)
    pl.semaphore_wait(barrier, len(partners))
    halo = [
        remote(geometry.at[pl.ds(OWN - REACH, REACH)], geo_halo.at[0], halo_send.at[0], halo_receive.at[0], above),
        remote(geometry.at[pl.ds(0, REACH)], geo_halo.at[1], halo_send.at[1], halo_receive.at[1], below),
        remote(charges_far.at[pl.ds(OWN - REACH, REACH)], ch_halo.at[0], halo_send.at[2], halo_receive.at[2], above),
        remote(charges_far.at[pl.ds(0, REACH)], ch_halo.at[1], halo_send.at[3], halo_receive.at[3], below),
    ]
    for copy in halo:
        copy.start()
    lax.fori_loop(1, 8, box_moments, 0)
    boxes = jnp.concatenate([moments[b] for b in range(8)], axis=1)
    top = dot3(boxes, box_transfer[...].reshape(8 * RANK, RANK), NN)
    own = [row_in(part, chip, core) for part in range(3)]
    gathered[0, own[0]] = boxes[:, :128]
    gathered[1, own[1]] = boxes[:, 128:]
    gathered[2, own[2]] = jnp.concatenate([top, jnp.zeros((RHS, 128 - RANK), f32)], axis=1)

    everything = list(halo)
    waiting = []
    for stage in range(3):
        size = 4**stage
        running = []
        for part in range(3):
            axis = ORDERS[part][stage]
            first = (own[part] // size) * size
            block = gathered.at[part, pl.ds(first, size)]
            for step in (1, 2, 3):
                slot = 3 * stage + step - 1
                copy = remote(block, block, send.at[part, slot], receive.at[part, slot], peer(axis, step))
                copy.start()
                running.append((part, step, copy))
            if stage == 2:
                copy = remote(block, block, send.at[part, 9], receive.at[part, 9], sibling)
                copy.start()
                waiting.append(copy)
        for part, step, copy in running:
            copy.wait_recv()
            if stage == 2:
                axis = ORDERS[part][2]
                third = (chip[axis] + 4 - step) % 4
                block = gathered.at[part, pl.ds((core * 4 + third) * 16, 16)]
                forward = remote(block, block, send.at[part, 9 + step], receive.at[part, 9 + step], sibling)
                forward.start()
                waiting.append(forward)
            everything.append(copy)
    for copy in waiting:
        copy.wait_recv()
    for copy in halo:
        copy.wait_recv()
    for copy in everything + waiting:
        copy.wait_send()


def exchange(geometry, charges, basis, leaf_transfer, box_transfer):
    far = pl.BlockSpec(memory_space=pl.ANY)
    vmem = pl.BlockSpec(memory_space=pltpu.VMEM)
    return pl.pallas_call(
        exchange_kernel,
        out_shape=(
            jax.ShapeDtypeStruct((3, 128, RHS, 128), f32),
            jax.ShapeDtypeStruct((2, REACH, 4, LEAF), f32),
            jax.ShapeDtypeStruct((2, REACH, RHS, LEAF), f32),
        ),
        in_specs=[far, far, vmem, vmem, vmem, vmem],
        out_specs=(vmem, far, far),
        scratch_shapes=[
            pltpu.VMEM((8, RHS, RANK), f32),
            pltpu.SemaphoreType.DMA((3, 13)),
            pltpu.SemaphoreType.DMA((3, 13)),
            pltpu.SemaphoreType.DMA((4,)),
            pltpu.SemaphoreType.DMA((4,)),
        ],
        compiler_params=pltpu.CompilerParams(vmem_limit_bytes=VMEM, collective_id=0, has_side_effects=True),
        name="exchange",
    )(geometry, charges, charges, basis, leaf_transfer, box_transfer)


def near_kernel(
    near_list, near_count, geometry, geo_halo, charges, ch_halo,
    out, geo, source, source_rows, target_rows, block_hi, block_lo, total, extent,
):
    offset = lax.axis_index(AXES) * OWN - REACH
    geo[0:REACH] = geo_halo[0]
    geo[REACH : REACH + OWN] = geometry[...]
    geo[REACH + OWN :] = geo_halo[1]
    centre = jnp.broadcast_to(jnp.mean(geometry[OWN // 2], axis=1, keepdims=True), (4, LEAF))
    one = jnp.ones((1, LEAF), f32)
    rest = jnp.zeros((3, LEAF), f32)

    def squared_norm(v):
        return v[0:1] * v[0:1] + v[1:2] * v[1:2] + v[2:3] * v[2:3]

    def weigh(part, start):
        def leaf(n, carry):
            area = geo[start + n][3:4] * (1.0 / FOUR_PI)
            hi, lo = halves(part[n] * area)
            source[start + n] = jnp.concatenate([hi, lo], axis=0)
            return carry

        lax.fori_loop(0, part.shape[0], leaf, 0, unroll=8)

    weigh(ch_halo.at[0], 0)
    weigh(charges, REACH)
    weigh(ch_halo.at[1], REACH + OWN)

    def target(n, largest):
        v = geo[n + REACH] - centre
        norm = squared_norm(v)
        a, b, c = thirds(jnp.concatenate([v[0:3], one, norm + SOFTENING, rest], axis=0))
        target_rows[n] = jnp.concatenate([a, a, b, b, a, c], axis=0).astype(bf16)
        total[n] = jnp.zeros((RHS, LEAF), f32)
        return jnp.maximum(largest, norm)

    def neighbour(n, largest):
        v = geo[n] - centre
        norm = squared_norm(v)
        a, b, c = thirds(jnp.concatenate([-2.0 * v[0:3], norm, one, rest], axis=0))
        source_rows[n, :, :FEATURES] = jnp.concatenate([a, b, a, b, c, a], axis=0).astype(bf16).T
        leaf = offset + n
        held = (leaf >= 0) & (leaf < lax.axis_size(AXES) * OWN)
        return jnp.maximum(largest, jnp.where(held, norm, 0.0))

    nothing = jnp.zeros((1, LEAF), f32)
    targets = lax.fori_loop(0, OWN, target, nothing, unroll=8)
    sources = lax.fori_loop(0, WIDE, neighbour, nothing, unroll=8)
    total[OWN] = jnp.zeros((RHS, LEAF), f32)
    extent[0] = jnp.max(targets) + jnp.max(sources)
    compact = extent[0] <= EXTENT

    @pl.when(compact)
    def _():
        pairs = lax.fori_loop(0, OWN, lambda n, s: s + near_count[n], 0)

        def after(leaf, slot):
            row = jnp.minimum(leaf, OWN - 1)
            more = slot + 1 < near_count[row]
            return jnp.where(more, leaf, jnp.minimum(leaf + 1, OWN)), jnp.where(more, slot + 1, 0)

        def fill(u, leaf, slot):
            row = jnp.minimum(leaf, OWN - 1)
            j = near_list[row, slot] - offset
            for q in range(0, LEAF, 128):
                entries = lax.rsqrt(dot(source_rows[j, q : q + 128, :FEATURES], target_rows[row], NN))
                hi, lo = halves(entries)
                block_hi[u, q : q + 128] = hi
                block_lo[u, q : q + 128] = lo
            return j

        def use(u, leaf, j):
            both = source[j]
            r = dot(both, block_hi[u], NN)
            total[leaf] = total[leaf] + (r[:RHS] + r[RHS:] + dot(both[:RHS], block_lo[u], NN))

        def round_of(state, use_old):
            leaf, slot = state[0], state[1]
            new = []
            for u in range(UNROLL):
                if use_old:
                    use(u, state[2 + 2 * u], state[3 + 2 * u])
                new += [leaf, fill(u, leaf, slot)]
                leaf, slot = after(leaf, slot)
            return (leaf, slot, *new)

        start = round_of((jnp.int32(0), jnp.int32(0)), False)
        lax.fori_loop(0, (pairs + UNROLL - 1) // UNROLL, lambda t, s: round_of(s, True), start)

    @pl.when(jnp.logical_not(compact))
    def _():
        def leaf_sum(n, carry):
            columns = geo[n + REACH].T

            def slot_sum(k, running):
                j = near_list[n, k] - offset
                v = geo[j]
                both = source[j]
                parts = []
                for p in range(0, LEAF, 128):
                    squared = jnp.full((128, LEAF), SOFTENING, f32)
                    for comp in range(3):
                        apart = columns[p : p + 128, comp : comp + 1] - v[comp : comp + 1]
                        squared = squared + apart * apart
                    hi, lo = halves(lax.rsqrt(squared))
                    r = dot(both, hi, NT)
                    parts.append(r[:RHS] + r[RHS:] + dot(both[:RHS], lo, NT))
                return running + jnp.concatenate(parts, axis=1)

            total[n] = lax.fori_loop(0, near_count[n], slot_sum, jnp.zeros((RHS, LEAF), f32))
            return carry

        lax.fori_loop(0, OWN, leaf_sum, 0)

    out[...] = total[0:OWN]


def near_field(near_list, near_count, *arrays):
    smem = pl.BlockSpec(memory_space=pltpu.SMEM)
    vmem = pl.BlockSpec(memory_space=pltpu.VMEM)
    return pl.pallas_call(
        near_kernel,
        out_shape=jax.ShapeDtypeStruct((OWN, RHS, LEAF), f32),
        in_specs=[smem] * 2 + [vmem] * 4,
        out_specs=vmem,
        scratch_shapes=[
            pltpu.VMEM((WIDE, 4, LEAF), f32),
            pltpu.VMEM((WIDE, 2 * RHS, LEAF), bf16),
            pltpu.VMEM((WIDE, LEAF, 128), bf16),
            pltpu.VMEM((OWN, FEATURES, LEAF), bf16),
            pltpu.VMEM((UNROLL, LEAF, LEAF), bf16),
            pltpu.VMEM((UNROLL, LEAF, LEAF), bf16),
            pltpu.VMEM((OWN + 1, RHS, LEAF), f32),
            pltpu.SMEM((1,), f32),
        ],
        compiler_params=pltpu.CompilerParams(vmem_limit_bytes=VMEM),
        cost_estimate=pl.CostEstimate(flops=2 * 10**10, bytes_accessed=4 * 10**6, transcendentals=5 * 10**7),
        name="near_field",
    )(near_list, near_count, *arrays)


def downward_kernel(
    box_far_list, top_far_list, gathered, top_coupling, box_transfer, box_coupling, leaf_transfer, basis, near,
    out, box_down,
):
    box = pl.program_id(0)

    @pl.when(box == 0)
    def _():
        top_local = jnp.zeros((RHS, RANK), f32)
        for f in range(FAR):
            chip, core = coordinates(top_far_list[0, f])
            top = gathered[2, row_in(2, chip, core), :, :RANK]
            top_local = top_local + dot3(top, top_coupling[0, f], NN)
        down = dot3(top_local, box_transfer[...].reshape(8 * RANK, RANK), NT)
        for b in range(8):
            box_down[b] = down[:, b * RANK : (b + 1) * RANK]

    local = box_down[box]
    for f in range(FAR):
        far = box_far_list[box, f]
        chip, core = coordinates(far // 8)
        part = (far % 8) // 4
        row = jnp.where(part == 0, row_in(0, chip, core), row_in(1, chip, core))
        tile = pltpu.roll(gathered[part, row], (4 - far % 4) % 4 * RANK, 1)
        local = local + dot3(tile[:, :RANK], box_coupling[0, f], NN)
    leaves = dot3(local, leaf_transfer[...].reshape(8 * RANK, RANK), NT)
    for c in range(8):
        out[c] = near[c] + dot3(leaves[:, c * RANK : (c + 1) * RANK], basis[c], NN)


def downward(box_far_list, top_far_list, gathered, top_coupling, box_transfer, box_coupling, leaf_transfer, basis, near):
    smem = pl.BlockSpec(memory_space=pltpu.SMEM)
    vmem = pl.BlockSpec(memory_space=pltpu.VMEM)
    return pl.pallas_call(
        downward_kernel,
        grid=(8,),
        out_shape=jax.ShapeDtypeStruct((OWN, RHS, LEAF), f32),
        in_specs=[
            smem,
            smem,
            vmem,
            vmem,
            vmem,
            pl.BlockSpec((1, FAR, RANK, RANK), lambda b: (b, 0, 0, 0)),
            pl.BlockSpec((1, 8, RANK, RANK), lambda b: (b, 0, 0, 0)),
            pl.BlockSpec((8, RANK, LEAF), lambda b: (b, 0, 0)),
            pl.BlockSpec((8, RHS, LEAF), lambda b: (b, 0, 0)),
        ],
        out_specs=pl.BlockSpec((8, RHS, LEAF), lambda b: (b, 0, 0)),
        scratch_shapes=[pltpu.VMEM((8, RHS, RANK), f32)],
        compiler_params=pltpu.CompilerParams(vmem_limit_bytes=VMEM),
        name="downward",
    )(box_far_list, top_far_list, gathered, top_coupling, box_transfer, box_coupling, leaf_transfer, basis, near)


def on_device(
    geometry,
    charges,
    leaf_cluster_basis,
    near_list,
    near_count,
    leaf_transfer,
    box_transfer,
    box_far_list,
    box_coupling,
    top_far_list,
    top_coupling,
):
    gathered, geo_halo, ch_halo = exchange(geometry, charges, leaf_cluster_basis, leaf_transfer, box_transfer)
    near = near_field(near_list, near_count, geometry, geo_halo, charges, ch_halo)
    return downward(
        box_far_list, top_far_list, gathered, top_coupling, box_transfer, box_coupling, leaf_transfer,
        leaf_cluster_basis, near,
    )


def solution(mesh):
    wide = P(AXES)
    return jax.shard_map(on_device, mesh=mesh, in_specs=(wide,) * 11, out_specs=wide, check_vma=False)
```

```python
import functools
import math

import jax
import jax.numpy as jnp
from jax import lax
from jax.experimental import pallas as pl
from jax.experimental.pallas import tpu as pltpu
from jax.sharding import PartitionSpec as P

SOFTENING = 0.0025
FOUR_PI = 4.0 * math.pi
AXES = ("group", "dev")

LEAF = 256
RANK = 32
RHS = 16
NEAR = 12
FAR = 16
REACH = 32
OWN = 64
WIDE = OWN + 2 * REACH
UNROLL = 16
VMEM = 60 * 2**20
FEATURES = 48
EXTENT = 8.0

f32 = jnp.float32
bf16 = jnp.bfloat16
NN = (((1,), (0,)), ((), ()))
NT = (((1,), (1,)), ((), ()))


def dot(a, b, dims):
    return lax.dot_general(a, b, dims, preferred_element_type=f32)


def halves(v):
    hi = v.astype(bf16)
    return hi, (v - hi.astype(f32)).astype(bf16)


def thirds(v):
    a = v.astype(bf16).astype(f32)
    b = (v - a).astype(bf16).astype(f32)
    return a, b, v - a - b


def dot3(a, b, dims):
    ah, al = halves(a)
    bh, bl = halves(b)
    rows = a.shape[0]
    both = dot(jnp.concatenate([ah, al], axis=0), bh, dims)
    return both[:rows] + both[rows:] + dot(ah, bl, dims)


ORDERS = ((0, 1, 2), (1, 2, 0), (2, 0, 1))


def coordinates(device):
    return (device >> 5, (device >> 1) & 3, (device >> 3) & 3), device & 1


def row_in(part, chip, core):
    first, second, third = (chip[axis] for axis in ORDERS[part])
    return (core << 6) + (third << 4) + (second << 2) + first


def exchange_kernel(
    geometry, charges_far, charges, basis, leaf_transfer, box_transfer,
    gathered, geo_halo, ch_halo, moments, send, receive, halo_send, halo_receive,
):
    me = lax.axis_index("group") * 32 + lax.axis_index("dev")
    chip, core = coordinates(me)

    def device(chip, core):
        return (chip[0], (chip[2] * 4 + chip[1]) * 2 + core)

    def peer(axis, step):
        moved = list(chip)
        moved[axis] = (chip[axis] + step) % 4
        return device(moved, core)

    sibling = device(chip, 1 - core)
    above = (me + 1) % 128
    below = (me + 127) % 128
    above = (above // 32, above % 32)
    below = (below // 32, below % 32)

    barrier = pltpu.get_barrier_semaphore()
    partners = [peer(axis, step) for axis in range(3) for step in (1, 2, 3)] + [sibling, above, below]
    for partner in partners:
        pl.semaphore_signal(barrier, inc=1, device_id=partner, device_id_type=pl.DeviceIdType.MESH)

    def remote(source, target, sent, received, partner):
        return pltpu.make_async_remote_copy(
            src_ref=source, dst_ref=target, send_sem=sent, recv_sem=received,
            device_id=partner, device_id_type=pl.DeviceIdType.MESH,
        )

    def box_moments(box, carry):
        parts = [dot3(charges[box * 8 + c], basis[box * 8 + c], NT) for c in range(8)]
        transfer = leaf_transfer[box].reshape(8 * RANK, RANK)
        moments[box] = dot3(jnp.concatenate(parts, axis=1), transfer, NN)
        return carry

    box_moments(0, 0)
    pl.semaphore_wait(barrier, len(partners))
    halo = [
        remote(geometry.at[pl.ds(OWN - REACH, REACH)], geo_halo.at[0], halo_send.at[0], halo_receive.at[0], above),
        remote(geometry.at[pl.ds(0, REACH)], geo_halo.at[1], halo_send.at[1], halo_receive.at[1], below),
        remote(charges_far.at[pl.ds(OWN - REACH, REACH)], ch_halo.at[0], halo_send.at[2], halo_receive.at[2], above),
        remote(charges_far.at[pl.ds(0, REACH)], ch_halo.at[1], halo_send.at[3], halo_receive.at[3], below),
    ]
    for copy in halo:
        copy.start()
    lax.fori_loop(1, 8, box_moments, 0)
    boxes = jnp.concatenate([moments[b] for b in range(8)], axis=1)
    top = dot3(boxes, box_transfer[...].reshape(8 * RANK, RANK), NN)
    own = [row_in(part, chip, core) for part in range(3)]
    gathered[0, own[0]] = boxes[:, :128]
    gathered[1, own[1]] = boxes[:, 128:]
    gathered[2, own[2]] = jnp.concatenate([top, jnp.zeros((RHS, 128 - RANK), f32)], axis=1)

    everything = list(halo)
    waiting = []
    for stage in range(3):
        size = 4**stage
        running = []
        for part in range(3):
            axis = ORDERS[part][stage]
            first = (own[part] // size) * size
            block = gathered.at[part, pl.ds(first, size)]
            for step in (1, 2, 3):
                slot = 3 * stage + step - 1
                copy = remote(block, block, send.at[part, slot], receive.at[part, slot], peer(axis, step))
                copy.start()
                running.append((part, step, copy))
            if stage == 2:
                copy = remote(block, block, send.at[part, 9], receive.at[part, 9], sibling)
                copy.start()
                waiting.append(copy)
        for part, step, copy in running:
            copy.wait_recv()
            if stage == 2:
                axis = ORDERS[part][2]
                third = (chip[axis] + 4 - step) % 4
                block = gathered.at[part, pl.ds((core * 4 + third) * 16, 16)]
                forward = remote(block, block, send.at[part, 9 + step], receive.at[part, 9 + step], sibling)
                forward.start()
                waiting.append(forward)
            everything.append(copy)
    for copy in waiting:
        copy.wait_recv()
    for copy in halo:
        copy.wait_recv()
    for copy in everything + waiting:
        copy.wait_send()


def exchange(geometry, charges, basis, leaf_transfer, box_transfer):
    far = pl.BlockSpec(memory_space=pl.ANY)
    vmem = pl.BlockSpec(memory_space=pltpu.VMEM)
    return pl.pallas_call(
        exchange_kernel,
        out_shape=(
            jax.ShapeDtypeStruct((3, 128, RHS, 128), f32),
            jax.ShapeDtypeStruct((2, REACH, 4, LEAF), f32),
            jax.ShapeDtypeStruct((2, REACH, RHS, LEAF), f32),
        ),
        in_specs=[far, far, vmem, vmem, vmem, vmem],
        out_specs=(vmem, far, far),
        scratch_shapes=[
            pltpu.VMEM((8, RHS, RANK), f32),
            pltpu.SemaphoreType.DMA((3, 13)),
            pltpu.SemaphoreType.DMA((3, 13)),
            pltpu.SemaphoreType.DMA((4,)),
            pltpu.SemaphoreType.DMA((4,)),
        ],
        compiler_params=pltpu.CompilerParams(vmem_limit_bytes=VMEM, collective_id=0, has_side_effects=True),
        name="exchange",
    )(geometry, charges, charges, basis, leaf_transfer, box_transfer)


def local_kernel(
    near_list, near_count, box_far_list, top_far_list, geometry, geo_halo, charges, ch_halo,
    gathered_far, top_coupling_far, box_transfer_far, box_coupling_far, leaf_transfer_far, basis_far,
    out, geo, source, source_rows, target_rows, block_hi, block_lo, total, extent,
    gathered, top_coupling, box_transfer, box_coupling, leaf_transfer, basis, arrived,
):
    loads = [
        pltpu.make_async_copy(far, here, arrived.at[n])
        for n, (far, here) in enumerate((
            (gathered_far, gathered), (top_coupling_far, top_coupling), (box_transfer_far, box_transfer),
            (box_coupling_far, box_coupling), (leaf_transfer_far, leaf_transfer), (basis_far, basis),
        ))
    ]
    for load in loads:
        load.start()
    offset = lax.axis_index(AXES) * OWN - REACH
    geo[0:REACH] = geo_halo[0]
    geo[REACH : REACH + OWN] = geometry[...]
    geo[REACH + OWN :] = geo_halo[1]
    centre = jnp.broadcast_to(jnp.mean(geometry[OWN // 2], axis=1, keepdims=True), (4, LEAF))
    one = jnp.ones((1, LEAF), f32)
    rest = jnp.zeros((3, LEAF), f32)

    def squared_norm(v):
        return v[0:1] * v[0:1] + v[1:2] * v[1:2] + v[2:3] * v[2:3]

    def weigh(part, start):
        def leaf(n, carry):
            area = geo[start + n][3:4] * (1.0 / FOUR_PI)
            hi, lo = halves(part[n] * area)
            source[start + n] = jnp.concatenate([hi, lo], axis=0)
            return carry

        lax.fori_loop(0, part.shape[0], leaf, 0, unroll=8)

    weigh(ch_halo.at[0], 0)
    weigh(charges, REACH)
    weigh(ch_halo.at[1], REACH + OWN)

    def target(n, largest):
        v = geo[n + REACH] - centre
        norm = squared_norm(v)
        a, b, c = thirds(jnp.concatenate([v[0:3], one, norm + SOFTENING, rest], axis=0))
        target_rows[n] = jnp.concatenate([a, a, b, b, a, c], axis=0).astype(bf16)
        total[n] = jnp.zeros((RHS, LEAF), f32)
        return jnp.maximum(largest, norm)

    def neighbour(n, largest):
        v = geo[n] - centre
        norm = squared_norm(v)
        a, b, c = thirds(jnp.concatenate([-2.0 * v[0:3], norm, one, rest], axis=0))
        source_rows[n, :, :FEATURES] = jnp.concatenate([a, b, a, b, c, a], axis=0).astype(bf16).T
        leaf = offset + n
        held = (leaf >= 0) & (leaf < lax.axis_size(AXES) * OWN)
        return jnp.maximum(largest, jnp.where(held, norm, 0.0))

    nothing = jnp.zeros((1, LEAF), f32)
    targets = lax.fori_loop(0, OWN, target, nothing, unroll=8)
    sources = lax.fori_loop(0, WIDE, neighbour, nothing, unroll=8)
    total[OWN] = jnp.zeros((RHS, LEAF), f32)
    extent[0] = jnp.max(targets) + jnp.max(sources)
    compact = extent[0] <= EXTENT

    @pl.when(compact)
    def _():
        pairs = lax.fori_loop(0, OWN, lambda n, s: s + near_count[n], 0)

        def after(leaf, slot):
            row = jnp.minimum(leaf, OWN - 1)
            more = slot + 1 < near_count[row]
            return jnp.where(more, leaf, jnp.minimum(leaf + 1, OWN)), jnp.where(more, slot + 1, 0)

        def fill(u, leaf, slot):
            row = jnp.minimum(leaf, OWN - 1)
            j = near_list[row, slot] - offset
            for q in range(0, LEAF, 128):
                entries = lax.rsqrt(dot(source_rows[j, q : q + 128, :FEATURES], target_rows[row], NN))
                hi, lo = halves(entries)
                block_hi[u, q : q + 128] = hi
                block_lo[u, q : q + 128] = lo
            return j

        def use(u, leaf, j):
            both = source[j]
            r = dot(both, block_hi[u], NN)
            total[leaf] = total[leaf] + (r[:RHS] + r[RHS:] + dot(both[:RHS], block_lo[u], NN))

        def round_of(state, use_old):
            leaf, slot = state[0], state[1]
            new = []
            for u in range(UNROLL):
                if use_old:
                    use(u, state[2 + 2 * u], state[3 + 2 * u])
                new += [leaf, fill(u, leaf, slot)]
                leaf, slot = after(leaf, slot)
            return (leaf, slot, *new)

        start = round_of((jnp.int32(0), jnp.int32(0)), False)
        lax.fori_loop(0, (pairs + UNROLL - 1) // UNROLL, lambda t, s: round_of(s, True), start)

    @pl.when(jnp.logical_not(compact))
    def _():
        def leaf_sum(n, carry):
            columns = geo[n + REACH].T

            def slot_sum(k, running):
                j = near_list[n, k] - offset
                v = geo[j]
                both = source[j]
                parts = []
                for p in range(0, LEAF, 128):
                    squared = jnp.full((128, LEAF), SOFTENING, f32)
                    for comp in range(3):
                        apart = columns[p : p + 128, comp : comp + 1] - v[comp : comp + 1]
                        squared = squared + apart * apart
                    hi, lo = halves(lax.rsqrt(squared))
                    r = dot(both, hi, NT)
                    parts.append(r[:RHS] + r[RHS:] + dot(both[:RHS], lo, NT))
                return running + jnp.concatenate(parts, axis=1)

            total[n] = lax.fori_loop(0, near_count[n], slot_sum, jnp.zeros((RHS, LEAF), f32))
            return carry

        lax.fori_loop(0, OWN, leaf_sum, 0)

    for load in loads:
        load.wait()
    downward(
        box_far_list, top_far_list, gathered, top_coupling, box_transfer, box_coupling, leaf_transfer, basis, total, out
    )


def picked(rows, lane):
    tiles = []
    for g in range(0, FAR, 4):
        tile = rows[g + 3]
        for k in (2, 1, 0):
            tile = jnp.where(lane < (k + 1) * RANK, rows[g + k], tile)
        tiles.append(tile)
    return jnp.concatenate(tiles, axis=1)


def downward(
    box_far_list, top_far_list, gathered, top_coupling, box_transfer, box_coupling, leaf_transfer, basis, total, out
):
    lane = lax.broadcasted_iota(jnp.int32, (RHS, 128), 1)
    rows = []
    for f in range(FAR):
        chip, core = coordinates(top_far_list[0, f])
        tile = gathered[2, row_in(2, chip, core)]
        rows.append(pltpu.roll(tile, f % 4 * RANK, 1) if f % 4 else tile)
    top_local = dot3(picked(rows, lane), top_coupling[0].reshape(FAR * RANK, RANK), NN)
    down = dot3(top_local, box_transfer[0].reshape(8 * RANK, RANK), NT)
    for box in range(8):
        rows = []
        for f in range(FAR):
            far = box_far_list[box, f]
            chip, core = coordinates(far >> 3)
            part = (far >> 2) & 1
            row = jnp.where(part == 0, row_in(0, chip, core), row_in(1, chip, core))
            rows.append(pltpu.roll(gathered[part, row], ((f - far) & 3) * RANK, 1))
        local = dot3(picked(rows, lane), box_coupling[box].reshape(FAR * RANK, RANK), NN)
        local = local + down[:, box * RANK : (box + 1) * RANK]
        leaves = dot3(local, leaf_transfer[box].reshape(8 * RANK, RANK), NT)
        for c in range(8):
            hi, lo = halves(leaves[:, c * RANK : (c + 1) * RANK])
            base, rest = halves(basis[8 * box + c])
            out[8 * box + c] = total[8 * box + c] + dot(
                jnp.concatenate([hi, lo, hi], axis=1), jnp.concatenate([base, base, rest], axis=0), NN
            )


def local_part(*arrays):
    smem = pl.BlockSpec(memory_space=pltpu.SMEM)
    vmem = pl.BlockSpec(memory_space=pltpu.VMEM)
    far = pl.BlockSpec(memory_space=pl.ANY)
    return pl.pallas_call(
        local_kernel,
        out_shape=jax.ShapeDtypeStruct((OWN, RHS, LEAF), f32),
        in_specs=[smem] * 4 + [vmem] * 4 + [far] * 6,
        out_specs=vmem,
        scratch_shapes=[
            pltpu.VMEM((WIDE, 4, LEAF), f32),
            pltpu.VMEM((WIDE, 2 * RHS, LEAF), bf16),
            pltpu.VMEM((WIDE, LEAF, 128), bf16),
            pltpu.VMEM((OWN, FEATURES, LEAF), bf16),
            pltpu.VMEM((UNROLL, LEAF, LEAF), bf16),
            pltpu.VMEM((UNROLL, LEAF, LEAF), bf16),
            pltpu.VMEM((OWN + 1, RHS, LEAF), f32),
            pltpu.SMEM((1,), f32),
        ]
        + [pltpu.VMEM(array.shape, f32) for array in arrays[8:]]
        + [pltpu.SemaphoreType.DMA((6,))],
        compiler_params=pltpu.CompilerParams(vmem_limit_bytes=VMEM),
        name="local_part",
    )(*arrays)


def on_device(
    geometry,
    charges,
    leaf_cluster_basis,
    near_list,
    near_count,
    leaf_transfer,
    box_transfer,
    box_far_list,
    box_coupling,
    top_far_list,
    top_coupling,
):
    gathered, geo_halo, ch_halo = exchange(geometry, charges, leaf_cluster_basis, leaf_transfer, box_transfer)
    return local_part(
        near_list, near_count, box_far_list, top_far_list, geometry, geo_halo, charges, ch_halo,
        gathered, top_coupling, box_transfer, box_coupling, leaf_transfer, leaf_cluster_basis,
    )


def solution(mesh):
    wide = P(AXES)
    return jax.shard_map(on_device, mesh=mesh, in_specs=(wide,) * 11, out_specs=wide, check_vma=False)
```

```python
import functools
import math

import jax
import jax.numpy as jnp
from jax import lax
from jax.experimental import pallas as pl
from jax.experimental.pallas import tpu as pltpu
from jax.sharding import PartitionSpec as P

SOFTENING = 0.0025
FOUR_PI = 4.0 * math.pi
AXES = ("group", "dev")

LEAF = 256
RANK = 32
RHS = 16
NEAR = 12
FAR = 16
REACH = 32
OWN = 64
WIDE = OWN + 2 * REACH
UNROLL = 16
VMEM = 60 * 2**20
FEATURES = 48
EXTENT = 8.0

f32 = jnp.float32
bf16 = jnp.bfloat16
NN = (((1,), (0,)), ((), ()))
NT = (((1,), (1,)), ((), ()))


def dot(a, b, dims):
    return lax.dot_general(a, b, dims, preferred_element_type=f32)


def halves(v):
    hi = v.astype(bf16)
    return hi, (v - hi.astype(f32)).astype(bf16)


def thirds(v):
    a = v.astype(bf16).astype(f32)
    b = (v - a).astype(bf16).astype(f32)
    return a, b, v - a - b


def dot3(a, b, dims):
    ah, al = halves(a)
    bh, bl = halves(b)
    rows = a.shape[0]
    both = dot(jnp.concatenate([ah, al], axis=0), bh, dims)
    return both[:rows] + both[rows:] + dot(ah, bl, dims)


ORDERS = ((0, 1, 2), (1, 2, 0), (2, 0, 1))


OWN_BLOCKS = (8, 0, 24, 24, 8)
HALO_PIECES = (0, 0, 0, 0, 1, 1, 1, 1)


def coordinates(device):
    return (device >> 5, (device >> 1) & 3, (device >> 3) & 3), device & 1


def row_in(part, chip, core):
    first, second, third = (chip[axis] for axis in ORDERS[part])
    return (core << 6) + (third << 4) + (second << 2) + first


def exchange_kernel(
    geometry_far, charges_far, geometry, charges, basis, leaf_transfer, box_transfer,
    gathered, geo_halo, ch_halo, partial, moments, send, receive, halo_send, halo_receive,
):
    me = lax.axis_index("group") * 32 + lax.axis_index("dev")
    chip, core = coordinates(me)

    def device(chip, core):
        return (chip[0], (chip[2] * 4 + chip[1]) * 2 + core)

    def peer(*moves):
        moved = list(chip)
        for axis, step in moves:
            moved[axis] = (chip[axis] + step) & 3
        return device(moved, core)

    sibling = device(chip, 1 - core)
    above = (me + 1) & 127
    below = (me + 127) & 127
    above = (above >> 5, above & 31)
    below = (below >> 5, below & 31)
    steps = [(one, two) for one in range(4) for two in range(4) if one or two]
    partners = [peer((axis, step)) for axis in range(3) for step in (1, 2, 3)]
    partners += [
        peer((first, one), (second, two)) for first, second, _ in ORDERS for one in (1, 2, 3) for two in (1, 2, 3)
    ]
    partners += [sibling, above, below]

    barrier = pltpu.get_barrier_semaphore()
    for partner in partners:
        pl.semaphore_signal(barrier, inc=1, device_id=partner, device_id_type=pl.DeviceIdType.MESH)

    def remote(source, target, sent, received, partner):
        return pltpu.make_async_remote_copy(
            src_ref=source, dst_ref=target, send_sem=sent, recv_sem=received,
            device_id=partner, device_id_type=pl.DeviceIdType.MESH,
        )

    def box_moments(box, carry):
        parts = [dot3(charges[box * 8 + c], basis[box * 8 + c], NT) for c in range(8)]
        transfer = leaf_transfer[box].reshape(8 * RANK, RANK)
        moments[box] = dot3(jnp.concatenate(parts, axis=1), transfer, NN)
        return carry

    def own_block(n, carry):
        here = geometry[n]
        hi, lo = halves(charges[n] * (here[3:4] * (1.0 / FOUR_PI)))
        both = jnp.concatenate([hi, lo], axis=0)
        columns = here.T
        total = jnp.zeros((RHS, LEAF), f32)
        for q in range(0, LEAF, 128):
            squared = jnp.full((128, LEAF), SOFTENING, f32)
            for comp in range(3):
                apart = columns[q : q + 128, comp : comp + 1] - here[comp : comp + 1]
                squared = squared + apart * apart
            hi, lo = halves(lax.rsqrt(squared))
            r = dot(both[:, q : q + 128], hi, NN)
            total = total + (r[:RHS] + r[RHS:] + dot(both[:RHS, q : q + 128], lo, NN))
        partial[n] = total
        return carry

    def own_blocks(point):
        first = sum(OWN_BLOCKS[:point])
        if OWN_BLOCKS[point]:
            lax.fori_loop(first, first + OWN_BLOCKS[point], own_block, 0, unroll=4)

    own_blocks(0)
    pl.semaphore_wait(barrier, len(partners))
    halo = []

    def start_halo(source, target, first, count, slot):
        for side, (begin, partner) in enumerate(((OWN - REACH, above), (0, below))):
            copy = remote(
                source.at[pl.ds(begin + first, count)], target.at[side, pl.ds(first, count)],
                halo_send.at[side, slot], halo_receive.at[side, slot], partner,
            )
            copy.start()
            halo.append(copy)

    def start_pieces(n):
        for piece in range(len(HALO_PIECES)):
            if HALO_PIECES[piece] == n:
                start_halo(charges_far, ch_halo, 4 * piece, 4, piece)

    start_halo(geometry_far, geo_halo, 0, REACH, 8)
    start_pieces(0)
    lax.fori_loop(0, 8, box_moments, 0)
    boxes = jnp.concatenate([moments[b] for b in range(8)], axis=1)
    top = dot3(boxes, box_transfer[...].reshape(8 * RANK, RANK), NN)
    own = [row_in(part, chip, core) for part in range(3)]
    gathered[0, own[0]] = boxes[:, :128]
    gathered[1, own[1]] = boxes[:, 128:]
    gathered[2, own[2]] = jnp.concatenate([top, jnp.zeros((RHS, 128 - RANK), f32)], axis=1)

    planes = []
    for part in range(3):
        first, second, _ = ORDERS[part]
        block = gathered.at[part, own[part]]
        for slot, (one, two) in enumerate(steps):
            copy = remote(block, block, send.at[part, slot], receive.at[part, slot], peer((first, one), (second, two)))
            copy.start()
            planes.append((part, copy))
    start_pieces(1)
    own_blocks(2)
    lines = []
    siblings = []
    for part in range(3):
        for of, copy in planes:
            if of == part:
                copy.wait_recv()
        third = ORDERS[part][2]
        block = gathered.at[part, pl.ds((core * 4 + chip[third]) * 16, 16)]
        for step in (1, 3, 2):
            slot = 14 + step
            copy = remote(block, block, send.at[part, slot], receive.at[part, slot], peer((third, step)))
            copy.start()
            lines.append((part, step, copy))
        copy = remote(block, block, send.at[part, 18], receive.at[part, 18], sibling)
        copy.start()
        siblings.append(copy)
    start_pieces(2)
    own_blocks(3)
    for part, step, copy in lines:
        copy.wait_recv()
        line = (chip[ORDERS[part][2]] + 4 - step) & 3
        block = gathered.at[part, pl.ds((core * 4 + line) * 16, 16)]
        forward = remote(block, block, send.at[part, 18 + step], receive.at[part, 18 + step], sibling)
        forward.start()
        siblings.append(forward)
    own_blocks(4)
    for copy in siblings + halo:
        copy.wait_recv()
    for copy in [copy for _, copy in planes] + [copy for _, _, copy in lines] + siblings + halo:
        copy.wait_send()


def exchange(geometry, charges, basis, leaf_transfer, box_transfer):
    far = pl.BlockSpec(memory_space=pl.ANY)
    vmem = pl.BlockSpec(memory_space=pltpu.VMEM)
    return pl.pallas_call(
        exchange_kernel,
        out_shape=(
            jax.ShapeDtypeStruct((3, 128, RHS, 128), f32),
            jax.ShapeDtypeStruct((2, REACH, 4, LEAF), f32),
            jax.ShapeDtypeStruct((2, REACH, RHS, LEAF), f32),
            jax.ShapeDtypeStruct((OWN, RHS, LEAF), f32),
        ),
        in_specs=[far, far, vmem, vmem, vmem, vmem, vmem],
        out_specs=(vmem, far, far, vmem),
        scratch_shapes=[
            pltpu.VMEM((8, RHS, RANK), f32),
            pltpu.SemaphoreType.DMA((3, 22)),
            pltpu.SemaphoreType.DMA((3, 22)),
            pltpu.SemaphoreType.DMA((2, 9)),
            pltpu.SemaphoreType.DMA((2, 9)),
        ],
        compiler_params=pltpu.CompilerParams(vmem_limit_bytes=VMEM, collective_id=0, has_side_effects=True),
        name="exchange",
    )(geometry, charges, geometry, charges, basis, leaf_transfer, box_transfer)


def local_kernel(
    near_list, near_count, box_far_list, top_far_list, geometry, geo_halo, charges, ch_halo, partial,
    gathered_far, top_coupling_far, box_transfer_far, box_coupling_far, leaf_transfer_far, basis_far,
    out, geo, source, source_rows, target_rows, block_hi, block_lo, total, extent, following,
    gathered, top_coupling, box_transfer, box_coupling, leaf_transfer, basis, arrived,
):
    loads = [
        pltpu.make_async_copy(far, here, arrived.at[n])
        for n, (far, here) in enumerate((
            (gathered_far, gathered), (top_coupling_far, top_coupling), (box_transfer_far, box_transfer),
            (box_coupling_far, box_coupling), (leaf_transfer_far, leaf_transfer), (basis_far, basis),
        ))
    ]
    for load in loads:
        load.start()
    offset = lax.axis_index(AXES) * OWN - REACH
    geo[0:REACH] = geo_halo[0]
    geo[REACH : REACH + OWN] = geometry[...]
    geo[REACH + OWN :] = geo_halo[1]
    centre = jnp.broadcast_to(jnp.mean(geometry[OWN // 2], axis=1, keepdims=True), (4, LEAF))
    one = jnp.ones((1, LEAF), f32)
    rest = jnp.zeros((3, LEAF), f32)

    def squared_norm(v):
        return v[0:1] * v[0:1] + v[1:2] * v[1:2] + v[2:3] * v[2:3]

    def weigh(part, start):
        def leaf(n, carry):
            area = geo[start + n][3:4] * (1.0 / FOUR_PI)
            hi, lo = halves(part[n] * area)
            source[start + n] = jnp.concatenate([hi, lo], axis=0)
            return carry

        lax.fori_loop(0, part.shape[0], leaf, 0, unroll=8)

    weigh(ch_halo.at[0], 0)
    weigh(charges, REACH)
    weigh(ch_halo.at[1], REACH + OWN)

    def target(n, largest):
        v = geo[n + REACH] - centre
        norm = squared_norm(v)
        a, b, c = thirds(jnp.concatenate([v[0:3], one, norm + SOFTENING, rest], axis=0))
        target_rows[n] = jnp.concatenate([a, a, b, b, a, c], axis=0).astype(bf16)
        total[n] = partial[n]
        return jnp.maximum(largest, norm)

    def neighbour(n, largest):
        v = geo[n] - centre
        norm = squared_norm(v)
        a, b, c = thirds(jnp.concatenate([-2.0 * v[0:3], norm, one, rest], axis=0))
        source_rows[n, :, :FEATURES] = jnp.concatenate([a, b, a, b, c, a], axis=0).astype(bf16).T
        leaf = offset + n
        held = (leaf >= 0) & (leaf < lax.axis_size(AXES) * OWN)
        return jnp.maximum(largest, jnp.where(held, norm, 0.0))

    nothing = jnp.zeros((1, LEAF), f32)
    targets = lax.fori_loop(0, OWN, target, nothing, unroll=8)
    sources = lax.fori_loop(0, WIDE, neighbour, nothing, unroll=8)
    total[OWN] = jnp.zeros((RHS, LEAF), f32)
    extent[0] = jnp.max(targets) + jnp.max(sources)
    compact = extent[0] <= EXTENT

    @pl.when(compact)
    def _():
        pairs = lax.fori_loop(0, OWN, lambda n, s: s + near_count[n] - 1, 0)

        def after(leaf, slot):
            row = jnp.minimum(leaf, OWN - 1)
            more = slot + 1 < near_count[row]
            return jnp.where(more, leaf, following[leaf]), jnp.where(more, slot + 1, 1)

        def back(n, next_leaf):
            leaf = OWN - 1 - n
            following[leaf] = next_leaf
            return jnp.where(near_count[leaf] > 1, leaf, next_leaf)

        following[OWN] = jnp.int32(OWN)
        first = lax.fori_loop(0, OWN, back, jnp.int32(OWN))

        def fill(u, leaf, slot):
            row = jnp.minimum(leaf, OWN - 1)
            j = near_list[row, slot] - offset
            for q in range(0, LEAF, 128):
                entries = lax.rsqrt(dot(source_rows[j, q : q + 128, :FEATURES], target_rows[row], NN))
                hi, lo = halves(entries)
                block_hi[u, q : q + 128] = hi
                block_lo[u, q : q + 128] = lo
            return j

        def use(u, leaf, j):
            both = source[j]
            r = dot(both, block_hi[u], NN)
            total[leaf] = total[leaf] + (r[:RHS] + r[RHS:] + dot(both[:RHS], block_lo[u], NN))

        def round_of(state, use_old):
            leaf, slot = state[0], state[1]
            new = []
            for u in range(UNROLL):
                if use_old:
                    use(u, state[2 + 2 * u], state[3 + 2 * u])
                new += [leaf, fill(u, leaf, slot)]
                leaf, slot = after(leaf, slot)
            return (leaf, slot, *new)

        start = round_of((first, jnp.int32(1)), False)
        lax.fori_loop(0, (pairs + UNROLL - 1) // UNROLL, lambda t, s: round_of(s, True), start)

    @pl.when(jnp.logical_not(compact))
    def _():
        def leaf_sum(n, carry):
            columns = geo[n + REACH].T

            def slot_sum(k, running):
                j = near_list[n, k] - offset
                v = geo[j]
                both = source[j]
                parts = []
                for p in range(0, LEAF, 128):
                    squared = jnp.full((128, LEAF), SOFTENING, f32)
                    for comp in range(3):
                        apart = columns[p : p + 128, comp : comp + 1] - v[comp : comp + 1]
                        squared = squared + apart * apart
                    hi, lo = halves(lax.rsqrt(squared))
                    r = dot(both, hi, NT)
                    parts.append(r[:RHS] + r[RHS:] + dot(both[:RHS], lo, NT))
                return running + jnp.concatenate(parts, axis=1)

            total[n] = lax.fori_loop(1, near_count[n], slot_sum, partial[n])
            return carry

        lax.fori_loop(0, OWN, leaf_sum, 0)

    for load in loads:
        load.wait()
    downward(
        box_far_list, top_far_list, gathered, top_coupling, box_transfer, box_coupling, leaf_transfer, basis, total, out
    )


def picked(rows, lane):
    tiles = []
    for g in range(0, FAR, 4):
        tile = rows[g + 3]
        for k in (2, 1, 0):
            tile = jnp.where(lane < (k + 1) * RANK, rows[g + k], tile)
        tiles.append(tile)
    return jnp.concatenate(tiles, axis=1)


def downward(
    box_far_list, top_far_list, gathered, top_coupling, box_transfer, box_coupling, leaf_transfer, basis, total, out
):
    lane = lax.broadcasted_iota(jnp.int32, (RHS, 128), 1)
    rows = []
    for f in range(FAR):
        chip, core = coordinates(top_far_list[0, f])
        tile = gathered[2, row_in(2, chip, core)]
        rows.append(pltpu.roll(tile, f % 4 * RANK, 1) if f % 4 else tile)
    top_local = dot3(picked(rows, lane), top_coupling[0].reshape(FAR * RANK, RANK), NN)
    down = dot3(top_local, box_transfer[0].reshape(8 * RANK, RANK), NT)
    for box in range(8):
        rows = []
        for f in range(FAR):
            far = box_far_list[box, f]
            chip, core = coordinates(far >> 3)
            part = (far >> 2) & 1
            row = jnp.where(part == 0, row_in(0, chip, core), row_in(1, chip, core))
            rows.append(pltpu.roll(gathered[part, row], ((f - far) & 3) * RANK, 1))
        local = dot3(picked(rows, lane), box_coupling[box].reshape(FAR * RANK, RANK), NN)
        local = local + down[:, box * RANK : (box + 1) * RANK]
        leaves = dot3(local, leaf_transfer[box].reshape(8 * RANK, RANK), NT)
        for c in range(8):
            hi, lo = halves(leaves[:, c * RANK : (c + 1) * RANK])
            base, rest = halves(basis[8 * box + c])
            out[8 * box + c] = total[8 * box + c] + dot(
                jnp.concatenate([hi, lo, hi], axis=1), jnp.concatenate([base, base, rest], axis=0), NN
            )


def local_part(*arrays):
    smem = pl.BlockSpec(memory_space=pltpu.SMEM)
    vmem = pl.BlockSpec(memory_space=pltpu.VMEM)
    far = pl.BlockSpec(memory_space=pl.ANY)
    return pl.pallas_call(
        local_kernel,
        out_shape=jax.ShapeDtypeStruct((OWN, RHS, LEAF), f32),
        in_specs=[smem] * 4 + [vmem] * 5 + [far] * 6,
        out_specs=vmem,
        scratch_shapes=[
            pltpu.VMEM((WIDE, 4, LEAF), f32),
            pltpu.VMEM((WIDE, 2 * RHS, LEAF), bf16),
            pltpu.VMEM((WIDE, LEAF, 128), bf16),
            pltpu.VMEM((OWN, FEATURES, LEAF), bf16),
            pltpu.VMEM((UNROLL, LEAF, LEAF), bf16),
            pltpu.VMEM((UNROLL, LEAF, LEAF), bf16),
            pltpu.VMEM((OWN + 1, RHS, LEAF), f32),
            pltpu.SMEM((1,), f32),
            pltpu.SMEM((OWN + 1,), jnp.int32),
        ]
        + [pltpu.VMEM(array.shape, f32) for array in arrays[9:]]
        + [pltpu.SemaphoreType.DMA((6,))],
        compiler_params=pltpu.CompilerParams(vmem_limit_bytes=VMEM),
        name="local_part",
    )(*arrays)


def on_device(
    geometry,
    charges,
    leaf_cluster_basis,
    near_list,
    near_count,
    leaf_transfer,
    box_transfer,
    box_far_list,
    box_coupling,
    top_far_list,
    top_coupling,
):
    gathered, geo_halo, ch_halo, partial = exchange(geometry, charges, leaf_cluster_basis, leaf_transfer, box_transfer)
    return local_part(
        near_list, near_count, box_far_list, top_far_list, geometry, geo_halo, charges, ch_halo, partial,
        gathered, top_coupling, box_transfer, box_coupling, leaf_transfer, leaf_cluster_basis,
    )


def solution(mesh):
    wide = P(AXES)
    return jax.shard_map(on_device, mesh=mesh, in_specs=(wide,) * 11, out_specs=wide, check_vma=False)
```

```python
import functools
import math

import jax
import jax.numpy as jnp
from jax import lax
from jax.experimental import pallas as pl
from jax.experimental.pallas import tpu as pltpu
from jax.sharding import PartitionSpec as P

SOFTENING = 0.0025
FOUR_PI = 4.0 * math.pi
AXES = ("group", "dev")

LEAF = 256
RANK = 32
RHS = 16
NEAR = 12
FAR = 16
REACH = 32
OWN = 64
WIDE = OWN + 2 * REACH
UNROLL = 16
VMEM = 60 * 2**20
FEATURES = 48
EXTENT = 8.0

f32 = jnp.float32
bf16 = jnp.bfloat16
NN = (((1,), (0,)), ((), ()))
NT = (((1,), (1,)), ((), ()))


def dot(a, b, dims):
    return lax.dot_general(a, b, dims, preferred_element_type=f32)


def halves(v):
    hi = v.astype(bf16)
    return hi, (v - hi.astype(f32)).astype(bf16)


def thirds(v):
    a = v.astype(bf16).astype(f32)
    b = (v - a).astype(bf16).astype(f32)
    return a, b, v - a - b


def dot3(a, b, dims):
    ah, al = halves(a)
    bh, bl = halves(b)
    rows = a.shape[0]
    both = dot(jnp.concatenate([ah, al], axis=0), bh, dims)
    return both[:rows] + both[rows:] + dot(ah, bl, dims)


ORDERS = ((0, 1, 2), (1, 2, 0), (2, 0, 1))


OWN_BLOCKS = (8, 0, 24, 24, 8)
HALO_PIECES = (0, 0, 0, 1, 1, 1, 1, 1)


def coordinates(device):
    return (device >> 5, (device >> 1) & 3, (device >> 3) & 3), device & 1


def row_in(part, chip, core):
    first, second, third = (chip[axis] for axis in ORDERS[part])
    return (core << 6) + (third << 4) + (second << 2) + first


def exchange_kernel(
    geometry_far, charges_far, basis_far, leaf_transfer_far, box_transfer_far, geometry, charges,
    gathered, geo_halo, ch_halo, partial, moments, basis, leaf_transfer, box_transfer, arrived, send, receive, halo_send, halo_receive,
):
    loads = [
        pltpu.make_async_copy(basis_far, basis, arrived.at[0]),
        pltpu.make_async_copy(leaf_transfer_far, leaf_transfer, arrived.at[1]),
        pltpu.make_async_copy(box_transfer_far, box_transfer, arrived.at[2]),
    ]
    for load in loads:
        load.start()
    me = lax.axis_index("group") * 32 + lax.axis_index("dev")
    chip, core = coordinates(me)

    def device(chip, core):
        return (chip[0], (chip[2] * 4 + chip[1]) * 2 + core)

    def peer(*moves):
        moved = list(chip)
        for axis, step in moves:
            moved[axis] = (chip[axis] + step) & 3
        return device(moved, core)

    sibling = device(chip, 1 - core)
    above = (me + 1) & 127
    below = (me + 127) & 127
    above = (above >> 5, above & 31)
    below = (below >> 5, below & 31)
    steps = [(one, two) for one in range(4) for two in range(4) if one or two]
    partners = [peer((axis, step)) for axis in range(3) for step in (1, 2, 3)]
    partners += [
        peer((first, one), (second, two)) for first, second, _ in ORDERS for one in (1, 2, 3) for two in (1, 2, 3)
    ]
    partners += [sibling, above, below]

    barrier = pltpu.get_barrier_semaphore()
    for partner in partners:
        pl.semaphore_signal(barrier, inc=1, device_id=partner, device_id_type=pl.DeviceIdType.MESH)

    def remote(source, target, sent, received, partner):
        return pltpu.make_async_remote_copy(
            src_ref=source, dst_ref=target, send_sem=sent, recv_sem=received,
            device_id=partner, device_id_type=pl.DeviceIdType.MESH,
        )

    def box_moments(box, carry):
        parts = [dot3(charges[box * 8 + c], basis[box * 8 + c], NT) for c in range(8)]
        transfer = leaf_transfer[box].reshape(8 * RANK, RANK)
        moments[box] = dot3(jnp.concatenate(parts, axis=1), transfer, NN)
        return carry

    def own_block(n, carry):
        here = geometry[n]
        hi, lo = halves(charges[n] * (here[3:4] * (1.0 / FOUR_PI)))
        both = jnp.concatenate([hi, lo], axis=0)
        columns = here.T
        total = jnp.zeros((RHS, LEAF), f32)
        for q in range(0, LEAF, 128):
            squared = jnp.full((128, LEAF), SOFTENING, f32)
            for comp in range(3):
                apart = columns[q : q + 128, comp : comp + 1] - here[comp : comp + 1]
                squared = squared + apart * apart
            hi, lo = halves(lax.rsqrt(squared))
            r = dot(both[:, q : q + 128], hi, NN)
            total = total + (r[:RHS] + r[RHS:] + dot(both[:RHS, q : q + 128], lo, NN))
        partial[n] = total
        return carry

    def own_blocks(point):
        first = sum(OWN_BLOCKS[:point])
        if OWN_BLOCKS[point]:
            lax.fori_loop(first, first + OWN_BLOCKS[point], own_block, 0, unroll=4)

    own_blocks(0)
    pl.semaphore_wait(barrier, len(partners))
    halo = []

    def start_halo(source, target, first, count, slot):
        for side, (begin, partner) in enumerate(((OWN - REACH, above), (0, below))):
            copy = remote(
                source.at[pl.ds(begin + first, count)], target.at[side, pl.ds(first, count)],
                halo_send.at[side, slot], halo_receive.at[side, slot], partner,
            )
            copy.start()
            halo.append(copy)

    def start_pieces(n):
        for piece in range(len(HALO_PIECES)):
            if HALO_PIECES[piece] == n:
                start_halo(charges_far, ch_halo, 4 * piece, 4, piece)

    start_halo(geometry_far, geo_halo, 0, REACH, 8)
    start_pieces(0)
    for load in loads:
        load.wait()
    lax.fori_loop(0, 8, box_moments, 0)
    boxes = jnp.concatenate([moments[b] for b in range(8)], axis=1)
    top = dot3(boxes, box_transfer[...].reshape(8 * RANK, RANK), NN)
    own = [row_in(part, chip, core) for part in range(3)]
    gathered[0, own[0]] = boxes[:, :128]
    gathered[1, own[1]] = boxes[:, 128:]
    gathered[2, own[2]] = jnp.concatenate([top, jnp.zeros((RHS, 128 - RANK), f32)], axis=1)

    planes = []
    for part in range(3):
        first, second, _ = ORDERS[part]
        block = gathered.at[part, own[part]]
        for slot, (one, two) in enumerate(steps):
            copy = remote(block, block, send.at[part, slot], receive.at[part, slot], peer((first, one), (second, two)))
            copy.start()
            planes.append((part, copy))
    start_pieces(1)
    own_blocks(2)
    lines = []
    siblings = []
    for part in range(3):
        for of, copy in planes:
            if of == part:
                copy.wait_recv()
        third = ORDERS[part][2]
        block = gathered.at[part, pl.ds((core * 4 + chip[third]) * 16, 16)]
        for step in (1, 3, 2):
            slot = 14 + step
            copy = remote(block, block, send.at[part, slot], receive.at[part, slot], peer((third, step)))
            copy.start()
            lines.append((part, step, copy))
        copy = remote(block, block, send.at[part, 18], receive.at[part, 18], sibling)
        copy.start()
        siblings.append(copy)
    start_pieces(2)
    own_blocks(3)
    for part, step, copy in lines:
        copy.wait_recv()
        line = (chip[ORDERS[part][2]] + 4 - step) & 3
        block = gathered.at[part, pl.ds((core * 4 + line) * 16, 16)]
        forward = remote(block, block, send.at[part, 18 + step], receive.at[part, 18 + step], sibling)
        forward.start()
        siblings.append(forward)
    own_blocks(4)
    for copy in siblings + halo:
        copy.wait_recv()
    for copy in [copy for _, copy in planes] + [copy for _, _, copy in lines] + siblings + halo:
        copy.wait_send()


def exchange(geometry, charges, basis, leaf_transfer, box_transfer):
    far = pl.BlockSpec(memory_space=pl.ANY)
    vmem = pl.BlockSpec(memory_space=pltpu.VMEM)
    return pl.pallas_call(
        exchange_kernel,
        out_shape=(
            jax.ShapeDtypeStruct((3, 128, RHS, 128), f32),
            jax.ShapeDtypeStruct((2, REACH, 4, LEAF), f32),
            jax.ShapeDtypeStruct((2, REACH, RHS, LEAF), f32),
            jax.ShapeDtypeStruct((OWN, RHS, LEAF), f32),
        ),
        in_specs=[far] * 5 + [vmem] * 2,
        out_specs=(vmem, far, far, vmem),
        scratch_shapes=[
            pltpu.VMEM((8, RHS, RANK), f32),
            pltpu.VMEM(basis.shape, f32),
            pltpu.VMEM(leaf_transfer.shape, f32),
            pltpu.VMEM(box_transfer.shape, f32),
            pltpu.SemaphoreType.DMA((3,)),
            pltpu.SemaphoreType.DMA((3, 22)),
            pltpu.SemaphoreType.DMA((3, 22)),
            pltpu.SemaphoreType.DMA((2, 9)),
            pltpu.SemaphoreType.DMA((2, 9)),
        ],
        compiler_params=pltpu.CompilerParams(vmem_limit_bytes=VMEM, collective_id=0, has_side_effects=True),
        name="exchange",
    )(geometry, charges, basis, leaf_transfer, box_transfer, geometry, charges)


def local_kernel(
    near_list_far, near_count, box_far_list, top_far_list, geometry, geo_halo, charges_far, ch_halo_far, partial,
    gathered_far, top_coupling_far, box_transfer_far, box_coupling_far, leaf_transfer_far, basis_far,
    out, geo, source, source_rows, target_rows, block_hi, block_lo, total, extent, following,
    gathered, top_coupling, box_transfer, box_coupling, leaf_transfer, basis, charges, ch_halo, near_list, arrived,
):
    loads = [
        pltpu.make_async_copy(far, here, arrived.at[n])
        for n, (far, here) in enumerate((
            (gathered_far, gathered), (top_coupling_far, top_coupling), (box_transfer_far, box_transfer),
            (box_coupling_far, box_coupling), (leaf_transfer_far, leaf_transfer), (basis_far, basis),
        ))
    ]
    early = [
        pltpu.make_async_copy(charges_far, charges, arrived.at[6]),
        pltpu.make_async_copy(ch_halo_far, ch_halo, arrived.at[7]),
        pltpu.make_async_copy(near_list_far, near_list, arrived.at[9]),
        pltpu.make_async_copy(partial, total.at[pl.ds(0, OWN)], arrived.at[8]),
    ]
    for load in early + loads:
        load.start()
    offset = lax.axis_index(AXES) * OWN - REACH
    geo[0:REACH] = geo_halo[0]
    geo[REACH : REACH + OWN] = geometry[...]
    geo[REACH + OWN :] = geo_halo[1]
    centre = jnp.broadcast_to(jnp.mean(geometry[OWN // 2], axis=1, keepdims=True), (4, LEAF))
    one = jnp.ones((1, LEAF), f32)
    rest = jnp.zeros((3, LEAF), f32)

    def squared_norm(v):
        return v[0:1] * v[0:1] + v[1:2] * v[1:2] + v[2:3] * v[2:3]

    def weigh(part, start):
        def leaf(n, carry):
            area = geo[start + n][3:4] * (1.0 / FOUR_PI)
            hi, lo = halves(part[n] * area)
            source[start + n] = jnp.concatenate([hi, lo], axis=0)
            return carry

        lax.fori_loop(0, part.shape[0], leaf, 0, unroll=8)


    def target(n, largest):
        v = geo[n + REACH] - centre
        norm = squared_norm(v)
        a, b, c = thirds(jnp.concatenate([v[0:3], one, norm + SOFTENING, rest], axis=0))
        target_rows[n] = jnp.concatenate([a, a, b, b, a, c], axis=0).astype(bf16)
        return jnp.maximum(largest, norm)

    def neighbour(n, largest):
        v = geo[n] - centre
        norm = squared_norm(v)
        a, b, c = thirds(jnp.concatenate([-2.0 * v[0:3], norm, one, rest], axis=0))
        source_rows[n, :, :FEATURES] = jnp.concatenate([a, b, a, b, c, a], axis=0).astype(bf16).T
        leaf = offset + n
        held = (leaf >= 0) & (leaf < lax.axis_size(AXES) * OWN)
        return jnp.maximum(largest, jnp.where(held, norm, 0.0))

    nothing = jnp.zeros((1, LEAF), f32)
    targets = lax.fori_loop(0, OWN, target, nothing, unroll=8)
    sources = lax.fori_loop(0, WIDE, neighbour, nothing, unroll=16)
    for load in early:
        load.wait()
    weigh(ch_halo.at[0], 0)
    weigh(charges, REACH)
    weigh(ch_halo.at[1], REACH + OWN)
    total[OWN] = jnp.zeros((RHS, LEAF), f32)
    extent[0] = jnp.max(targets) + jnp.max(sources)
    compact = extent[0] <= EXTENT

    @pl.when(compact)
    def _():
        pairs = lax.fori_loop(0, OWN, lambda n, s: s + near_count[n] - 1, 0)

        def after(leaf, slot):
            row = jnp.minimum(leaf, OWN - 1)
            more = slot + 1 < near_count[row]
            return jnp.where(more, leaf, following[leaf]), jnp.where(more, slot + 1, 1)

        def back(n, next_leaf):
            leaf = OWN - 1 - n
            following[leaf] = next_leaf
            return jnp.where(near_count[leaf] > 1, leaf, next_leaf)

        following[OWN] = jnp.int32(OWN)
        first = lax.fori_loop(0, OWN, back, jnp.int32(OWN))

        def fill(u, leaf, slot):
            row = jnp.minimum(leaf, OWN - 1)
            j = near_list[row, slot] - offset
            for q in range(0, LEAF, 128):
                entries = lax.rsqrt(dot(source_rows[j, q : q + 128, :FEATURES], target_rows[row], NN))
                hi, lo = halves(entries)
                block_hi[u, q : q + 128] = hi
                block_lo[u, q : q + 128] = lo
            return j

        def use(u, leaf, j):
            both = source[j]
            r = dot(both, block_hi[u], NN)
            total[leaf] = total[leaf] + (r[:RHS] + r[RHS:] + dot(both[:RHS], block_lo[u], NN))

        def round_of(state, use_old):
            leaf, slot = state[0], state[1]
            new = []
            for u in range(UNROLL):
                if use_old:
                    use(u, state[2 + 2 * u], state[3 + 2 * u])
                new += [leaf, fill(u, leaf, slot)]
                leaf, slot = after(leaf, slot)
            return (leaf, slot, *new)

        start = round_of((first, jnp.int32(1)), False)
        lax.fori_loop(0, (pairs + UNROLL - 1) // UNROLL, lambda t, s: round_of(s, True), start)

    @pl.when(jnp.logical_not(compact))
    def _():
        def leaf_sum(n, carry):
            columns = geo[n + REACH].T

            def slot_sum(k, running):
                j = near_list[n, k] - offset
                v = geo[j]
                both = source[j]
                parts = []
                for p in range(0, LEAF, 128):
                    squared = jnp.full((128, LEAF), SOFTENING, f32)
                    for comp in range(3):
                        apart = columns[p : p + 128, comp : comp + 1] - v[comp : comp + 1]
                        squared = squared + apart * apart
                    hi, lo = halves(lax.rsqrt(squared))
                    r = dot(both, hi, NT)
                    parts.append(r[:RHS] + r[RHS:] + dot(both[:RHS], lo, NT))
                return running + jnp.concatenate(parts, axis=1)

            total[n] = lax.fori_loop(1, near_count[n], slot_sum, total[n])
            return carry

        lax.fori_loop(0, OWN, leaf_sum, 0)

    for load in loads:
        load.wait()
    downward(
        box_far_list, top_far_list, gathered, top_coupling, box_transfer, box_coupling, leaf_transfer, basis, total, out
    )


def picked(rows, lane):
    tiles = []
    for g in range(0, FAR, 4):
        tile = rows[g + 3]
        for k in (2, 1, 0):
            tile = jnp.where(lane < (k + 1) * RANK, rows[g + k], tile)
        tiles.append(tile)
    return jnp.concatenate(tiles, axis=1)


def downward(
    box_far_list, top_far_list, gathered, top_coupling, box_transfer, box_coupling, leaf_transfer, basis, total, out
):
    lane = lax.broadcasted_iota(jnp.int32, (RHS, 128), 1)
    rows = []
    for f in range(FAR):
        chip, core = coordinates(top_far_list[0, f])
        tile = gathered[2, row_in(2, chip, core)]
        rows.append(pltpu.roll(tile, f % 4 * RANK, 1) if f % 4 else tile)
    top_local = dot3(picked(rows, lane), top_coupling[0].reshape(FAR * RANK, RANK), NN)
    down = dot3(top_local, box_transfer[0].reshape(8 * RANK, RANK), NT)
    for box in range(8):
        rows = []
        for f in range(FAR):
            far = box_far_list[box, f]
            chip, core = coordinates(far >> 3)
            part = (far >> 2) & 1
            row = jnp.where(part == 0, row_in(0, chip, core), row_in(1, chip, core))
            rows.append(pltpu.roll(gathered[part, row], ((f - far) & 3) * RANK, 1))
        local = dot3(picked(rows, lane), box_coupling[box].reshape(FAR * RANK, RANK), NN)
        local = local + down[:, box * RANK : (box + 1) * RANK]
        leaves = dot3(local, leaf_transfer[box].reshape(8 * RANK, RANK), NT)
        for c in range(8):
            hi, lo = halves(leaves[:, c * RANK : (c + 1) * RANK])
            base, rest = halves(basis[8 * box + c])
            out[8 * box + c] = total[8 * box + c] + dot(
                jnp.concatenate([hi, lo, hi], axis=1), jnp.concatenate([base, base, rest], axis=0), NN
            )


def local_part(*arrays):
    smem = pl.BlockSpec(memory_space=pltpu.SMEM)
    vmem = pl.BlockSpec(memory_space=pltpu.VMEM)
    far = pl.BlockSpec(memory_space=pl.ANY)
    return pl.pallas_call(
        local_kernel,
        out_shape=jax.ShapeDtypeStruct((OWN, RHS, LEAF), f32),
        in_specs=[far] + [smem] * 3 + [vmem] * 2 + [far] * 9,
        out_specs=vmem,
        scratch_shapes=[
            pltpu.VMEM((WIDE, 4, LEAF), f32),
            pltpu.VMEM((WIDE, 2 * RHS, LEAF), bf16),
            pltpu.VMEM((WIDE, LEAF, 128), bf16),
            pltpu.VMEM((OWN, FEATURES, LEAF), bf16),
            pltpu.VMEM((UNROLL, LEAF, LEAF), bf16),
            pltpu.VMEM((UNROLL, LEAF, LEAF), bf16),
            pltpu.VMEM((OWN + 1, RHS, LEAF), f32),
            pltpu.SMEM((1,), f32),
            pltpu.SMEM((OWN + 1,), jnp.int32),
        ]
        + [pltpu.VMEM(array.shape, f32) for array in arrays[9:]]
        + [pltpu.VMEM(arrays[n].shape, f32) for n in (6, 7)]
        + [pltpu.SMEM((OWN, NEAR), jnp.int32)]
        + [pltpu.SemaphoreType.DMA((10,))],
        compiler_params=pltpu.CompilerParams(vmem_limit_bytes=VMEM),
        name="local_part",
    )(*arrays)


def on_device(
    geometry,
    charges,
    leaf_cluster_basis,
    near_list,
    near_count,
    leaf_transfer,
    box_transfer,
    box_far_list,
    box_coupling,
    top_far_list,
    top_coupling,
):
    gathered, geo_halo, ch_halo, partial = exchange(geometry, charges, leaf_cluster_basis, leaf_transfer, box_transfer)
    return local_part(
        near_list, near_count, box_far_list, top_far_list, geometry, geo_halo, charges, ch_halo, partial,
        gathered, top_coupling, box_transfer, box_coupling, leaf_transfer, leaf_cluster_basis,
    )


def solution(mesh):
    wide = P(AXES)
    return jax.shard_map(on_device, mesh=mesh, in_specs=(wide,) * 11, out_specs=wide, check_vma=False)
```

```python
import functools
import math

import jax
import jax.numpy as jnp
from jax import lax
from jax.experimental import pallas as pl
from jax.experimental.pallas import tpu as pltpu
from jax.sharding import PartitionSpec as P

SOFTENING = 0.0025
FOUR_PI = 4.0 * math.pi
AXES = ("group", "dev")

LEAF = 256
RANK = 32
RHS = 16
NEAR = 12
FAR = 16
REACH = 32
OWN = 64
WIDE = OWN + 2 * REACH
UNROLL = 16
VMEM = 60 * 2**20
FEATURES = 48
EXTENT = 8.0

f32 = jnp.float32
bf16 = jnp.bfloat16
NN = (((1,), (0,)), ((), ()))
NT = (((1,), (1,)), ((), ()))


def dot(a, b, dims):
    return lax.dot_general(a, b, dims, preferred_element_type=f32)


def halves(v):
    hi = v.astype(bf16)
    return hi, (v - hi.astype(f32)).astype(bf16)


def thirds(v):
    a = v.astype(bf16).astype(f32)
    b = (v - a).astype(bf16).astype(f32)
    return a, b, v - a - b


def dot3(a, b, dims):
    ah, al = halves(a)
    bh, bl = halves(b)
    rows = a.shape[0]
    both = dot(jnp.concatenate([ah, al], axis=0), bh, dims)
    return both[:rows] + both[rows:] + dot(ah, bl, dims)


ORDERS = ((0, 1, 2), (1, 2, 0), (2, 0, 1))


OWN_BLOCKS = (8, 0, 24, 24, 8)
HALO_PIECES = (0, 0, 0, 1, 1, 1, 1, 1)


def coordinates(device):
    return (device >> 5, (device >> 1) & 3, (device >> 3) & 3), device & 1


def row_in(part, chip, core):
    first, second, third = (chip[axis] for axis in ORDERS[part])
    return (core << 6) + (third << 4) + (second << 2) + first


def exchange_kernel(
    geometry_far, charges_far, basis_far, leaf_transfer_far, box_transfer_far, geometry, charges,
    gathered, geo_halo, ch_halo, partial, moments, basis, leaf_transfer, box_transfer, arrived, send, receive, halo_send, halo_receive,
):
    loads = [
        pltpu.make_async_copy(basis_far, basis, arrived.at[0]),
        pltpu.make_async_copy(leaf_transfer_far, leaf_transfer, arrived.at[1]),
        pltpu.make_async_copy(box_transfer_far, box_transfer, arrived.at[2]),
    ]
    for load in loads:
        load.start()
    me = lax.axis_index("group") * 32 + lax.axis_index("dev")
    chip, core = coordinates(me)

    def device(chip, core):
        return (chip[0], (chip[2] * 4 + chip[1]) * 2 + core)

    def peer(*moves):
        moved = list(chip)
        for axis, step in moves:
            moved[axis] = (chip[axis] + step) & 3
        return device(moved, core)

    sibling = device(chip, 1 - core)
    above = (me + 1) & 127
    below = (me + 127) & 127
    above = (above >> 5, above & 31)
    below = (below >> 5, below & 31)
    steps = [(one, two) for one in range(4) for two in range(4) if one or two]
    partners = [peer((axis, step)) for axis in range(3) for step in (1, 2, 3)]
    partners += [
        peer((first, one), (second, two)) for first, second, _ in ORDERS for one in (1, 2, 3) for two in (1, 2, 3)
    ]
    partners += [sibling, above, below]

    barrier = pltpu.get_barrier_semaphore()
    for partner in partners:
        pl.semaphore_signal(barrier, inc=1, device_id=partner, device_id_type=pl.DeviceIdType.MESH)

    def remote(source, target, sent, received, partner):
        return pltpu.make_async_remote_copy(
            src_ref=source, dst_ref=target, send_sem=sent, recv_sem=received,
            device_id=partner, device_id_type=pl.DeviceIdType.MESH,
        )

    def box_moments(box, carry):
        parts = [dot3(charges[box * 8 + c], basis[box * 8 + c], NT) for c in range(8)]
        transfer = leaf_transfer[box].reshape(8 * RANK, RANK)
        moments[box] = dot3(jnp.concatenate(parts, axis=1), transfer, NN)
        return carry

    def own_block(n, carry):
        here = geometry[n]
        hi, lo = halves(charges[n] * (here[3:4] * (1.0 / FOUR_PI)))
        both = jnp.concatenate([hi, lo], axis=0)
        columns = here.T
        total = jnp.zeros((RHS, LEAF), f32)
        for q in range(0, LEAF, 128):
            squared = jnp.full((128, LEAF), SOFTENING, f32)
            for comp in range(3):
                apart = columns[q : q + 128, comp : comp + 1] - here[comp : comp + 1]
                squared = squared + apart * apart
            hi, lo = halves(lax.rsqrt(squared))
            r = dot(both[:, q : q + 128], hi, NN)
            total = total + (r[:RHS] + r[RHS:] + dot(both[:RHS, q : q + 128], lo, NN))
        partial[n] = total
        return carry

    def own_blocks(point):
        first = sum(OWN_BLOCKS[:point])
        if OWN_BLOCKS[point]:
            lax.fori_loop(first, first + OWN_BLOCKS[point], own_block, 0, unroll=4)

    own_blocks(0)
    pl.semaphore_wait(barrier, len(partners))
    halo = []

    def start_halo(source, target, first, count, slot):
        for side, (begin, partner) in enumerate(((OWN - REACH, above), (0, below))):
            copy = remote(
                source.at[pl.ds(begin + first, count)], target.at[side, pl.ds(first, count)],
                halo_send.at[side, slot], halo_receive.at[side, slot], partner,
            )
            copy.start()
            halo.append(copy)

    def start_pieces(n):
        for piece in range(len(HALO_PIECES)):
            if HALO_PIECES[piece] == n:
                start_halo(charges_far, ch_halo, 4 * piece, 4, piece)

    start_halo(geometry_far, geo_halo, 0, REACH, 8)
    start_pieces(0)
    for load in loads:
        load.wait()
    lax.fori_loop(0, 8, box_moments, 0)
    boxes = jnp.concatenate([moments[b] for b in range(8)], axis=1)
    top = dot3(boxes, box_transfer[...].reshape(8 * RANK, RANK), NN)
    own = [row_in(part, chip, core) for part in range(3)]
    gathered[0, own[0]] = boxes[:, :128]
    gathered[1, own[1]] = boxes[:, 128:]
    gathered[2, own[2]] = jnp.concatenate([top, jnp.zeros((RHS, 128 - RANK), f32)], axis=1)

    planes = []
    for part in range(3):
        first, second, _ = ORDERS[part]
        block = gathered.at[part, own[part]]
        for slot, (one, two) in enumerate(steps):
            copy = remote(block, block, send.at[part, slot], receive.at[part, slot], peer((first, one), (second, two)))
            copy.start()
            planes.append((part, copy))
    start_pieces(1)
    own_blocks(2)
    lines = []
    siblings = []
    for part in range(3):
        for of, copy in planes:
            if of == part:
                copy.wait_recv()
        third = ORDERS[part][2]
        block = gathered.at[part, pl.ds((core * 4 + chip[third]) * 16, 16)]
        for step in (1, 3, 2):
            slot = 14 + step
            copy = remote(block, block, send.at[part, slot], receive.at[part, slot], peer((third, step)))
            copy.start()
            lines.append((part, step, copy))
        copy = remote(block, block, send.at[part, 18], receive.at[part, 18], sibling)
        copy.start()
        siblings.append(copy)
    start_pieces(2)
    own_blocks(3)
    for part, step, copy in lines:
        copy.wait_recv()
        line = (chip[ORDERS[part][2]] + 4 - step) & 3
        block = gathered.at[part, pl.ds((core * 4 + line) * 16, 16)]
        forward = remote(block, block, send.at[part, 18 + step], receive.at[part, 18 + step], sibling)
        forward.start()
        siblings.append(forward)
    own_blocks(4)
    for copy in siblings + halo:
        copy.wait_recv()
    for copy in [copy for _, copy in planes] + [copy for _, _, copy in lines] + siblings + halo:
        copy.wait_send()


def exchange(geometry, charges, basis, leaf_transfer, box_transfer):
    far = pl.BlockSpec(memory_space=pl.ANY)
    vmem = pl.BlockSpec(memory_space=pltpu.VMEM)
    return pl.pallas_call(
        exchange_kernel,
        out_shape=(
            jax.ShapeDtypeStruct((3, 128, RHS, 128), f32),
            jax.ShapeDtypeStruct((2, REACH, 4, LEAF), f32),
            jax.ShapeDtypeStruct((2, REACH, RHS, LEAF), f32),
            jax.ShapeDtypeStruct((OWN, RHS, LEAF), f32),
        ),
        in_specs=[far] * 5 + [vmem] * 2,
        out_specs=(vmem, far, far, vmem),
        scratch_shapes=[
            pltpu.VMEM((8, RHS, RANK), f32),
            pltpu.VMEM(basis.shape, f32),
            pltpu.VMEM(leaf_transfer.shape, f32),
            pltpu.VMEM(box_transfer.shape, f32),
            pltpu.SemaphoreType.DMA((3,)),
            pltpu.SemaphoreType.DMA((3, 22)),
            pltpu.SemaphoreType.DMA((3, 22)),
            pltpu.SemaphoreType.DMA((2, 9)),
            pltpu.SemaphoreType.DMA((2, 9)),
        ],
        compiler_params=pltpu.CompilerParams(vmem_limit_bytes=VMEM, collective_id=0, has_side_effects=True),
        name="exchange",
    )(geometry, charges, basis, leaf_transfer, box_transfer, geometry, charges)


def local_kernel(
    near_list_far, near_count, box_far_list, top_far_list, geometry, geo_halo, charges_far, ch_halo_far, partial,
    gathered_far, top_coupling_far, box_transfer_far, box_coupling_far, leaf_transfer_far, basis_far,
    out, geo, source, source_rows, target_rows, block_hi, block_lo, total, extent, following,
    gathered, top_coupling, box_transfer, box_coupling, leaf_transfer, basis, charges, ch_halo, near_list, arrived,
):
    loads = [
        pltpu.make_async_copy(far, here, arrived.at[n])
        for n, (far, here) in enumerate((
            (gathered_far, gathered), (top_coupling_far, top_coupling), (box_transfer_far, box_transfer),
            (box_coupling_far, box_coupling), (leaf_transfer_far, leaf_transfer), (basis_far, basis),
        ))
    ]
    early = [
        pltpu.make_async_copy(charges_far, charges, arrived.at[6]),
        pltpu.make_async_copy(ch_halo_far, ch_halo, arrived.at[7]),
        pltpu.make_async_copy(near_list_far, near_list, arrived.at[9]),
        pltpu.make_async_copy(partial, total.at[pl.ds(0, OWN)], arrived.at[8]),
    ]
    for load in early + loads:
        load.start()
    offset = lax.axis_index(AXES) * OWN - REACH
    geo[0:REACH] = geo_halo[0]
    geo[REACH : REACH + OWN] = geometry[...]
    geo[REACH + OWN :] = geo_halo[1]
    centre = jnp.broadcast_to(jnp.mean(geometry[OWN // 2], axis=1, keepdims=True), (4, LEAF))
    one = jnp.ones((1, LEAF), f32)
    rest = jnp.zeros((3, LEAF), f32)

    def squared_norm(v):
        return v[0:1] * v[0:1] + v[1:2] * v[1:2] + v[2:3] * v[2:3]

    def weigh(part, start):
        def leaf(n, carry):
            area = geo[start + n][3:4] * (1.0 / FOUR_PI)
            hi, lo = halves(part[n] * area)
            source[start + n] = jnp.concatenate([hi, lo], axis=0)
            return carry

        lax.fori_loop(0, part.shape[0], leaf, 0, unroll=8)


    def target(n, largest):
        v = geo[n + REACH] - centre
        norm = squared_norm(v)
        a, b, c = thirds(jnp.concatenate([v[0:3], one, norm + SOFTENING, rest], axis=0))
        target_rows[n] = jnp.concatenate([a, a, b, b, a, c], axis=0).astype(bf16)
        return jnp.maximum(largest, norm)

    def neighbour(n, largest):
        v = geo[n] - centre
        norm = squared_norm(v)
        a, b, c = thirds(jnp.concatenate([-2.0 * v[0:3], norm, one, rest], axis=0))
        source_rows[n, :, :FEATURES] = jnp.concatenate([a, b, a, b, c, a], axis=0).astype(bf16).T
        leaf = offset + n
        held = (leaf >= 0) & (leaf < lax.axis_size(AXES) * OWN)
        return jnp.maximum(largest, jnp.where(held, norm, 0.0))

    nothing = jnp.zeros((1, LEAF), f32)
    targets = lax.fori_loop(0, OWN, target, nothing, unroll=8)
    sources = lax.fori_loop(0, WIDE, neighbour, nothing, unroll=16)
    for load in early:
        load.wait()
    weigh(ch_halo.at[0], 0)
    weigh(charges, REACH)
    weigh(ch_halo.at[1], REACH + OWN)
    total[OWN] = jnp.zeros((RHS, LEAF), f32)
    extent[0] = jnp.max(targets) + jnp.max(sources)
    compact = extent[0] <= EXTENT

    @pl.when(compact)
    def _():
        pairs = lax.fori_loop(0, OWN, lambda n, s: s + near_count[n] - 1, 0)

        def after(leaf, slot):
            row = jnp.minimum(leaf, OWN - 1)
            more = slot + 1 < near_count[row]
            return jnp.where(more, leaf, following[leaf]), jnp.where(more, slot + 1, 1)

        def back(n, next_leaf):
            leaf = OWN - 1 - n
            following[leaf] = next_leaf
            return jnp.where(near_count[leaf] > 1, leaf, next_leaf)

        following[OWN] = jnp.int32(OWN)
        first = lax.fori_loop(0, OWN, back, jnp.int32(OWN))

        def fill(u, leaf, slot):
            row = jnp.minimum(leaf, OWN - 1)
            j = near_list[slot, row] - offset
            for q in range(0, LEAF, 128):
                entries = lax.rsqrt(dot(source_rows[j, q : q + 128, :FEATURES], target_rows[row], NN))
                hi, lo = halves(entries)
                block_hi[u, q : q + 128] = hi
                block_lo[u, q : q + 128] = lo
            return j

        def use(u, leaf, j):
            both = source[j]
            r = dot(both, block_hi[u], NN)
            total[leaf] = total[leaf] + (r[:RHS] + r[RHS:] + dot(both[:RHS], block_lo[u], NN))

        def round_of(state, use_old):
            leaf, slot = state[0], state[1]
            new = []
            for u in range(UNROLL):
                if use_old:
                    use(u, state[2 + 2 * u], state[3 + 2 * u])
                new += [leaf, fill(u, leaf, slot)]
                leaf, slot = after(leaf, slot)
            return (leaf, slot, *new)

        start = round_of((first, jnp.int32(1)), False)
        lax.fori_loop(0, (pairs + UNROLL - 1) // UNROLL, lambda t, s: round_of(s, True), start)

    @pl.when(jnp.logical_not(compact))
    def _():
        def leaf_sum(n, carry):
            columns = geo[n + REACH].T

            def slot_sum(k, running):
                j = near_list[k, n] - offset
                v = geo[j]
                both = source[j]
                parts = []
                for p in range(0, LEAF, 128):
                    squared = jnp.full((128, LEAF), SOFTENING, f32)
                    for comp in range(3):
                        apart = columns[p : p + 128, comp : comp + 1] - v[comp : comp + 1]
                        squared = squared + apart * apart
                    hi, lo = halves(lax.rsqrt(squared))
                    r = dot(both, hi, NT)
                    parts.append(r[:RHS] + r[RHS:] + dot(both[:RHS], lo, NT))
                return running + jnp.concatenate(parts, axis=1)

            total[n] = lax.fori_loop(1, near_count[n], slot_sum, total[n])
            return carry

        lax.fori_loop(0, OWN, leaf_sum, 0)

    for load in loads:
        load.wait()
    downward(
        box_far_list, top_far_list, gathered, top_coupling, box_transfer, box_coupling, leaf_transfer, basis, total, out
    )


def picked(rows, lane):
    tiles = []
    for g in range(0, FAR, 4):
        tile = rows[g + 3]
        for k in (2, 1, 0):
            tile = jnp.where(lane < (k + 1) * RANK, rows[g + k], tile)
        tiles.append(tile)
    return jnp.concatenate(tiles, axis=1)


def downward(
    box_far_list, top_far_list, gathered, top_coupling, box_transfer, box_coupling, leaf_transfer, basis, total, out
):
    lane = lax.broadcasted_iota(jnp.int32, (RHS, 128), 1)
    rows = []
    for f in range(FAR):
        chip, core = coordinates(top_far_list[0, f])
        tile = gathered[2, row_in(2, chip, core)]
        rows.append(pltpu.roll(tile, f % 4 * RANK, 1) if f % 4 else tile)
    top_local = dot3(picked(rows, lane), top_coupling[0].reshape(FAR * RANK, RANK), NN)
    down = dot3(top_local, box_transfer[0].reshape(8 * RANK, RANK), NT)
    for box in range(8):
        rows = []
        for f in range(FAR):
            far = box_far_list[box, f]
            chip, core = coordinates(far >> 3)
            part = (far >> 2) & 1
            row = jnp.where(part == 0, row_in(0, chip, core), row_in(1, chip, core))
            rows.append(pltpu.roll(gathered[part, row], ((f - far) & 3) * RANK, 1))
        local = dot3(picked(rows, lane), box_coupling[box].reshape(FAR * RANK, RANK), NN)
        local = local + down[:, box * RANK : (box + 1) * RANK]
        leaves = dot3(local, leaf_transfer[box].reshape(8 * RANK, RANK), NT)
        for c in range(8):
            hi, lo = halves(leaves[:, c * RANK : (c + 1) * RANK])
            base, rest = halves(basis[8 * box + c])
            out[8 * box + c] = total[8 * box + c] + dot(
                jnp.concatenate([hi, lo, hi], axis=1), jnp.concatenate([base, base, rest], axis=0), NN
            )


def local_part(*arrays):
    smem = pl.BlockSpec(memory_space=pltpu.SMEM)
    vmem = pl.BlockSpec(memory_space=pltpu.VMEM)
    far = pl.BlockSpec(memory_space=pl.ANY)
    return pl.pallas_call(
        local_kernel,
        out_shape=jax.ShapeDtypeStruct((OWN, RHS, LEAF), f32),
        in_specs=[far] + [smem] * 3 + [vmem] * 2 + [far] * 9,
        out_specs=vmem,
        scratch_shapes=[
            pltpu.VMEM((WIDE, 4, LEAF), f32),
            pltpu.VMEM((WIDE, 2 * RHS, LEAF), bf16),
            pltpu.VMEM((WIDE, LEAF, 128), bf16),
            pltpu.VMEM((OWN, FEATURES, LEAF), bf16),
            pltpu.VMEM((UNROLL, LEAF, LEAF), bf16),
            pltpu.VMEM((UNROLL, LEAF, LEAF), bf16),
            pltpu.VMEM((OWN + 1, RHS, LEAF), f32),
            pltpu.SMEM((1,), f32),
            pltpu.SMEM((OWN + 1,), jnp.int32),
        ]
        + [pltpu.VMEM(array.shape, f32) for array in arrays[9:]]
        + [pltpu.VMEM(arrays[n].shape, f32) for n in (6, 7)]
        + [pltpu.SMEM((NEAR, OWN), jnp.int32)]
        + [pltpu.SemaphoreType.DMA((10,))],
        compiler_params=pltpu.CompilerParams(vmem_limit_bytes=VMEM),
        name="local_part",
    )(*arrays)


def on_device(
    geometry,
    charges,
    leaf_cluster_basis,
    near_list,
    near_count,
    leaf_transfer,
    box_transfer,
    box_far_list,
    box_coupling,
    top_far_list,
    top_coupling,
):
    gathered, geo_halo, ch_halo, partial = exchange(geometry, charges, leaf_cluster_basis, leaf_transfer, box_transfer)
    return local_part(
        near_list.T, near_count, box_far_list, top_far_list, geometry, geo_halo, charges, ch_halo, partial,
        gathered, top_coupling, box_transfer, box_coupling, leaf_transfer, leaf_cluster_basis,
    )


def solution(mesh):
    wide = P(AXES)
    return jax.shard_map(on_device, mesh=mesh, in_specs=(wide,) * 11, out_specs=wide, check_vma=False)
```
